32 devices in a mesh: fsdp: 8 (over z, y), dp: 4 (over x, core).
Axes of the slice: x: 2, y: 2, z: 4, core: 2. Of those that a mesh axis runs over, the one named last changes fastest.
Arguments:
- byte_ids: int32 [32, 1024], P(('fsdp', 'dp')), may hold values from 0 to 255
- token_segments: int32 [32, 512], P(('fsdp', 'dp')), may hold values from 0 to 15, never falling along the last dimension, each value on 1 to 256 neighbouring positions
- embed: float32 [256, 768], P('fsdp'), may hold values from -6 to 6
- conv_w: float32 [4, 768], P(None, 'fsdp'), may hold values from -3 to 3
- conv_b: float32 [768], P('fsdp'), may hold values from -3 to 3
- score_w: float32 [768], P('fsdp'), may hold values from -0.4375 to 0.4375
- norm_attn: float32 [768], P('fsdp'), may hold values from 0.1 to 1.9
- w_query: float32 [768, 768], P('fsdp'), may hold values from -0.21875 to 0.21875
- w_key: float32 [768, 768], P('fsdp'), may hold values from -0.21875 to 0.21875
- w_value: float32 [768, 768], P('fsdp'), may hold values from -0.21875 to 0.21875
- w_out: float32 [768, 768], P('fsdp'), may hold values from -0.625 to 0.625
- rel_bias: float32 [384], P('fsdp'), may hold values from -4 to 4
- norm_ffn: float32 [768], P('fsdp'), may hold values from 0.1 to 1.9
- w_gate: float32 [768, 2048], P('fsdp'), may hold values from -0.21875 to 0.21875
- w_up: float32 [768, 2048], P('fsdp'), may hold values from -0.21875 to 0.21875
- w_down: float32 [2048, 768], P('fsdp'), may hold values from -0.125 to 0.125
- out_grad: bfloat16 [16384, 768], P(('fsdp', 'dp')), may hold values from -6 to 6
Outputs:
- mixed: bfloat16 [16384, 768], P(('fsdp', 'dp'))
- grad_embed: float32 [256, 768], P('fsdp')
- grad_conv_w: float32 [4, 768], P(None, 'fsdp')
- grad_conv_b: float32 [768], P('fsdp')
- grad_score_w: float32 [768], P('fsdp')
- grad_norm_attn: float32 [768], P('fsdp')
- grad_query: float32 [768, 768], P('fsdp')
- grad_key: float32 [768, 768], P('fsdp')
- grad_value: float32 [768, 768], P('fsdp')
- grad_out: float32 [768, 768], P('fsdp')
- grad_rel_bias: float32 [384], P('fsdp')
- grad_norm_ffn: float32 [768], P('fsdp')
- grad_gate: float32 [768, 2048], P('fsdp')
- grad_up: float32 [768, 2048], P('fsdp')
- grad_down: float32 [2048, 768], P('fsdp')
The draws below stay inside these ranges and needn't reach their ends.
Inputs may be any that keep to these rules, and one draw needn't show every extreme that they name: `token_segments`: in each row the segment numbers never fall and each segment holds 1 to 256 tokens.
All inputs are finite; a program needn't handle non-finite values.
Results may differ from the reference program's by a relative error of at most 0.02.
Values may be sent and summed in bfloat16 or wider, within the bound.
A program may use at most 320 MiB of HBM per device.

```python
import math
import jax
import jax.numpy as jnp
import numpy as np
from jax import lax

D = 768
HEADS = 12
HEAD_DIM = 64
FF = 2048
VOCAB = 256
BUCKETS = 32
ROW_TOK = 512
ROWS = 32
ROW_BYTES = 1024


def touch_ends(entries, key, smallest, largest):
    dims = entries.shape
    place = [jax.random.randint(jax.random.fold_in(key, axis), (), 0, dims[axis]) for axis in range(len(dims))]
    entries = entries.at[tuple(place)].set(smallest)
    longest = dims.index(max(dims))
    place[longest] = (place[longest] + 1) % dims[longest]
    return entries.at[tuple(place)].set(largest)


def levels(key, dims, pieces, least, high):
    def one(axis_at, parts):
        steps = jax.random.uniform(jax.random.fold_in(jax.random.fold_in(key, 6), axis_at), (parts,), jnp.float32, least / len(pieces), high / len(pieces))
        return jnp.repeat(jnp.exp(steps), dims[axis_at] // parts).reshape((-1,) + (1,) * (len(dims) - axis_at - 1))

    level = one(*pieces[0])
    for cut in pieces[1:]:
        level = level * one(*cut)
    return level


def rank_table(amount, slope):
    loads = [(1 << 20) // math.isqrt(rank ** slope) + 1 for rank in range(1, amount + 1)]
    width = 1 + sum(loads) // (1 << 30)
    return np.cumsum(np.array([max(1, weight // width) for weight in loads]))


def skewed_ids(rng, shape, amount, skew):
    grid = rank_table(amount, skew)
    pick = jax.random.randint(jax.random.fold_in(rng, 1), shape, 0, int(grid[amount - 1]))
    grade = jnp.searchsorted(jnp.asarray(grid, jnp.int32), pick, side="right")
    return jax.random.permutation(jax.random.fold_in(rng, 2), amount)[grade].astype(jnp.int32)


def split_up(number_of, total, limit, lean):
    loads = [(1 << 20) // math.isqrt(grade ** lean) + 1 for grade in range(2, number_of + 1)]
    spare, holding = total - limit - (number_of - 1), [1] * (number_of - 1)
    while spare > 0:
        free = [i for i in range(number_of - 1) if holding[i] < limit]
        mass, remaining = sum([loads[i] for i in free]), spare
        for i in free:
            extra = min(limit - holding[i], max(1, remaining * loads[i] // mass), spare)
            holding[i] = holding[i] + extra
            spare = spare - extra
    return np.array([limit] + holding)


def ragged(own_key, number_of, total, reach, lean):
    if number_of == 2:
        one = jax.random.randint(own_key, (), max(1, total - reach), min(reach, total - 1) + 1)
        return jnp.stack([one, total - one])
    lengths = jnp.asarray(split_up(number_of, total, reach, lean), jnp.int32)
    couples = (number_of - 1) // 2
    donor, receiver = lengths[1:1 + 2 * couples:2], lengths[2:2 + 2 * couples:2]
    slack = jnp.minimum(donor - 1, reach - receiver)
    moved = jax.random.randint(jax.random.fold_in(own_key, 1), (couples,), 0, 1 << 20) % (slack + 1)
    lengths = lengths.at[1:1 + 2 * couples:2].set(donor - moved).at[2:2 + 2 * couples:2].set(receiver + moved)
    return lengths[jax.random.permutation(jax.random.fold_in(own_key, 2), number_of)]


def normal_values(stream_key, shape, scale, most, split=(), held_as=jnp.bfloat16):
    factor_of = levels(stream_key, shape, split, -0.22, 0.18) if split else 1.0
    entries = jax.random.normal(stream_key, shape, jnp.float32) * scale * factor_of
    return jnp.minimum(jnp.maximum(entries, -most), most).astype(held_as)


def setup_inputs(seed: int = 0) -> dict:
    streams_of = jax.random.split(jax.random.key(seed), 18)
    byte_ids = touch_ends(skewed_ids(streams_of[0], (ROWS, ROW_BYTES), VOCAB, 2), jax.random.fold_in(streams_of[0], 3), 0, VOCAB - 1).astype(jnp.int32)
    token_segments = jax.vmap(lambda own: jnp.searchsorted(jnp.cumsum(ragged(own, 16, ROW_TOK, ROW_TOK // 2, 2)), jnp.arange(ROW_TOK), side="right"))(jax.random.split(streams_of[1], ROWS)).reshape((ROWS, ROW_TOK)).astype(jnp.int32)
    embed = normal_values(streams_of[2], (VOCAB, D), 1.0, 6.0, ((0, 8),), jnp.float32)
    conv_w = normal_values(streams_of[3], (4, D), 0.5, 3.0, ((1, 8),), jnp.float32)
    conv_b = normal_values(streams_of[4], (D,), 0.5, 3.0, ((0, 8),), jnp.float32)
    score_w = normal_values(streams_of[5], (D,), (D // 4) ** -0.5, 0.4375, ((0, 8),), jnp.float32)
    norm_attn = jnp.clip(1.0 + 0.18 * jax.random.normal(streams_of[6], (D,), jnp.float32), 0.1, 1.9)
    w_query = normal_values(streams_of[7], (D, D), D ** -0.5, 0.21875, ((0, 8),), jnp.float32)
    w_key = normal_values(streams_of[8], (D, D), D ** -0.5, 0.21875, ((0, 8),), jnp.float32)
    w_value = normal_values(streams_of[9], (D, D), D ** -0.5, 0.21875, ((0, 8),), jnp.float32)
    w_out = normal_values(streams_of[10], (D, D), (D // 8) ** -0.5, 0.625, ((0, 8),), jnp.float32)
    rel_bias = normal_values(streams_of[11], (BUCKETS * HEADS,), 1.0, 4.0, ((0, 8),), jnp.float32)
    norm_ffn = jnp.clip(1.0 + 0.18 * jax.random.normal(streams_of[12], (D,), jnp.float32), 0.1, 1.9)
    w_gate = normal_values(streams_of[13], (D, FF), D ** -0.5, 0.21875, ((0, 8),), jnp.float32)
    w_up = normal_values(streams_of[14], (D, FF), D ** -0.5, 0.21875, ((0, 8),), jnp.float32)
    w_down = normal_values(streams_of[15], (FF, D), FF ** -0.5, 0.125, ((0, 8),), jnp.float32)
    out_grad = normal_values(streams_of[16], (ROWS * ROW_TOK, D), 1.0, 6.0, ((0, 32),))
    return dict(byte_ids=byte_ids, token_segments=token_segments, embed=embed, conv_w=conv_w, conv_b=conv_b, score_w=score_w, norm_attn=norm_attn, w_query=w_query, w_key=w_key, w_value=w_value, w_out=w_out, rel_bias=rel_bias, norm_ffn=norm_ffn, w_gate=w_gate, w_up=w_up, w_down=w_down, out_grad=out_grad)


@jax.custom_vjp
def low(v):
    return lax.optimization_barrier(v.astype(jnp.bfloat16)).astype(jnp.float32)

@jax.custom_vjp
def low_back(v):
    return v

def low_keep(v):
    return (low(v), None)

def low_pass(kept, grad):
    return (grad,)

def back_keep(v):
    return (v, None)

def back_low(kept, grad):
    return (low(grad),)
low.defvjp(low_keep, low_pass)
low_back.defvjp(back_keep, back_low)
PRECISION = lax.Precision.HIGHEST
THRESHOLDS = (12, 16, 23, 32, 46, 64, 91)
EPSILON = 1e-06

def round_both(values):
    return low(low_back(values))

def product(left, right):
    return jnp.dot(left, right, precision=PRECISION, preferred_element_type=jnp.float32)

def shifted(array, offset):
    if offset == 0:
        return array
    filler = jnp.zeros((abs(offset),) + array.shape[1:], array.dtype)
    if offset > 0:
        return jnp.concatenate([array[offset:], filler], axis=0)
    return jnp.concatenate([filler, array[:offset]], axis=0)

def same_segment(segment, offset):
    marked = segment + 1
    return shifted(marked, offset) == marked

def gbst_block(byte_row, segment_tok, embed, conv_w, conv_b, score_w):
    length = byte_row.shape[0]
    segment = jnp.repeat(segment_tok, 2)
    one_hot = (byte_row[:, None] == jnp.arange(VOCAB, dtype=jnp.int32)[None, :]).astype(jnp.float32)
    embedded = low_back(product(one_hot, embed))
    conv_out = jnp.broadcast_to(conv_b[None, :], embedded.shape)
    for offset in range(-2, 2):
        inside = same_segment(segment, offset).astype(jnp.float32)
        conv_out = conv_out + conv_w[offset + 2][None, :] * shifted(embedded, offset) * inside[:, None]
    position = jnp.arange(length, dtype=jnp.int32)
    moved = {}
    matches = {}
    for offset in range(-3, 4):
        moved[offset] = shifted(conv_out, offset)
        matches[offset] = same_segment(segment, offset)
    pooled_all = []
    score_all = []
    for pool_size in range(1, 5):
        phase = position % pool_size
        total = jnp.zeros_like(conv_out)
        members = jnp.zeros((length,), jnp.float32)
        for offset in range(1 - pool_size, pool_size):
            taken = ((phase + offset >= 0) & (phase + offset < pool_size) & matches[offset]).astype(jnp.float32)
            total = total + taken[:, None] * moved[offset]
            members = members + taken
        pooled = total / members[:, None]
        pooled_all.append(pooled)
        score_all.append(lax.optimization_barrier(jnp.sum(pooled * score_w[None, :], axis=1)))
    weights_b = jax.nn.softmax(jnp.stack(score_all, axis=1), axis=1)
    combined = sum((weights_b[:, index:index + 1] * pooled_all[index] for index in range(4)))
    return lax.optimization_barrier(jnp.mean(combined.reshape(length // 2, 2, -1), axis=1))

def rms_norm(values, gain):
    return values * lax.rsqrt(lax.optimization_barrier(jnp.mean(values * values, axis=1, keepdims=True)) + EPSILON) * gain[None, :]

def bucket_of(relative):
    distance = jnp.abs(relative)
    far = 8 + sum(((distance >= threshold).astype(jnp.int32) for threshold in THRESHOLDS))
    return jnp.where(distance < 8, distance, far) + 16 * (relative > 0).astype(jnp.int32)

def offset_table(table, length):
    relative = jnp.arange(2 * length, dtype=jnp.int32) - (length - 1)
    one_hot = (bucket_of(relative)[:, None] == jnp.arange(BUCKETS, dtype=jnp.int32)[None, :]).astype(jnp.float32)
    return jnp.dot(one_hot, table, precision=lax.Precision.HIGHEST, preferred_element_type=jnp.float32)

def attend(queries, key_rows, value_rows, segment_tok, by_offset):
    head_count, length, head_width = queries.shape
    block_rows = min(512, length)
    block_count = length // block_rows
    span = length + block_rows
    grouped = queries.reshape(head_count, block_count, block_rows, head_width).transpose(1, 0, 2, 3)
    segments_q = segment_tok.reshape(block_count, block_rows)
    starts = jnp.arange(block_count, dtype=jnp.int32) * block_rows

    def one_block(inputs):
        query_block, segment_block, start = inputs
        raw = low_back(jnp.einsum('hqd,hkd->hqk', query_block, key_rows, precision=PRECISION, preferred_element_type=jnp.float32) * 0.125)
        nearby = lax.dynamic_slice_in_dim(by_offset, length - block_rows - start, span, 0).T
        spread = jnp.broadcast_to(nearby[:, None, :], (head_count, block_rows, span)).reshape(head_count, block_rows * span)
        bias = spread[:, block_rows - 1:block_rows - 1 + block_rows * (span - 1)]
        bias = bias.reshape(head_count, block_rows, span - 1)[:, :, :length]
        visible = segment_block[:, None] == segment_tok[None, :]
        probs = jax.nn.softmax(jnp.where(visible[None], raw + bias, -1000000000.0), axis=2)
        return jnp.einsum('hqk,hkd->hqd', low(probs), value_rows, precision=PRECISION, preferred_element_type=jnp.float32)
    outputs = lax.map(jax.checkpoint(one_block), (grouped, segments_q, starts))
    return outputs.transpose(0, 2, 1, 3).reshape(length, head_count * head_width)

def encoder(start_rows, segment_tok, params):
    norm_attn, w_query, w_key, w_value, w_out, rel_bias, norm_ffn, w_gate, w_up, w_down = params
    length = start_rows.shape[0]
    attn_in = low(rms_norm(start_rows, norm_attn))

    def split_heads(values):
        return values.reshape(length, HEADS, HEAD_DIM).transpose(1, 0, 2)
    queries = split_heads(round_both(product(attn_in, w_query)))
    key_rows = split_heads(round_both(product(attn_in, w_key)))
    value_rows = split_heads(round_both(product(attn_in, w_value)))
    by_offset = offset_table(rel_bias.reshape(BUCKETS, HEADS), length)
    context = round_both(attend(queries, key_rows, value_rows, segment_tok, by_offset))
    after_attn = start_rows + low_back(product(context, w_out))
    ffn_in = low(rms_norm(after_attn, norm_ffn))
    gate = low_back(product(ffn_in, w_gate))
    up_proj = low_back(product(ffn_in, w_up))
    hidden = low(jax.nn.gelu(gate, approximate=True) * up_proj)
    return after_attn + low_back(product(hidden, w_down))

def row_forward(params, byte_row, segment_tok):
    start_rows = gbst_block(byte_row, segment_tok, params[0], params[1], params[2], params[3])
    return encoder(start_rows, segment_tok, params[4:])

def reference(byte_ids, token_segments, embed, conv_w, conv_b, score_w, norm_attn, w_query, w_key, w_value, w_out, rel_bias, norm_ffn, w_gate, w_up, w_down, out_grad):
    params = (embed, conv_w, conv_b, score_w, norm_attn, w_query, w_key, w_value, w_out, rel_bias, norm_ffn, w_gate, w_up, w_down)

    def forward(weights_in):
        rounded = tuple((low(weight) for weight in weights_in))

        def one_row(state_in, inputs):
            return (state_in, row_forward(rounded, inputs[0], inputs[1]))
        return lax.scan(jax.checkpoint(one_row), jnp.zeros((), jnp.float32), (byte_ids, token_segments))[1]
    outputs, pullback = jax.vjp(forward, params)
    grads = pullback(out_grad.astype(jnp.float32).reshape(outputs.shape))[0]
    mixed = outputs.reshape(-1, D).astype(jnp.bfloat16)
    return (mixed, grads[0], grads[1], grads[2], grads[3], grads[4], grads[5], grads[6], grads[7], grads[8], grads[9], grads[10], grads[11], grads[12], grads[13])
```

```python
import functools
import jax
import jax.numpy as jnp
from jax import lax
from jax.experimental import pallas as pl
from jax.experimental.pallas import tpu as pltpu
from jax.sharding import PartitionSpec as P

F32 = jnp.float32
BF16 = jnp.bfloat16
I32 = jnp.int32
D = 768
FF = 2048
HEADS = 12
VOCAB = 256
BUCKETS = 32
TOK = 512
BYTES = 1024
PAD = 64
SPAN = BYTES + 2 * PAD
THRESHOLDS = (12, 16, 23, 32, 46, 64, 91)
EPSILON = 1e-06
MESH = pl.DeviceIdType.MESH


class Sizes:
    def __init__(self, shards):
        self.shards = shards
        self.emb = VOCAB // shards
        self.d = D // shards
        self.ff = FF // shards
        self.rel = BUCKETS * HEADS // shards


def nn(a, b):
    return jnp.dot(a, b, preferred_element_type=F32)


def nt(a, b):
    return lax.dot_general(a, b, (((1,), (1,)), ((), ())), preferred_element_type=F32)


def tn(a, b):
    return lax.dot_general(a, b, (((0,), (0,)), ((), ())), preferred_element_type=F32)


def iota(shape, dim):
    return lax.broadcasted_iota(I32, shape, dim)


def split3_rows(row):
    hi = row.astype(BF16).astype(F32)
    mid = (row - hi).astype(BF16).astype(F32)
    low = (row - hi - mid).astype(BF16).astype(F32)
    at = iota(row.shape, 0)
    zero = jnp.zeros_like(row)
    return jnp.where(at == 0, hi, jnp.where(at == 1, mid, jnp.where(at == 2, low, zero))).astype(BF16)


def expand_smalls(sz, small):
    wide = jnp.zeros((16, D), F32)
    flat = jnp.zeros((16, BUCKETS * HEADS), F32)
    for s in range(sz.shards):
        piece = small[s]
        i, c = iota((128, D), 0), iota((128, D), 1)
        place = jnp.where((c == i + s * sz.d) & (i < sz.d), 1.0, 0.0).astype(BF16)
        wide = wide + nn(piece, place)
        i, c = iota((128, BUCKETS * HEADS), 0), iota((128, BUCKETS * HEADS), 1)
        place = jnp.where((c == i + s * sz.rel) & (i < sz.rel), 1.0, 0.0).astype(BF16)
        flat = flat + nn(piece, place)
    return wide, flat


def bucket_of(relative):
    distance = jnp.abs(relative)
    far = jnp.full(relative.shape, 8, I32)
    for threshold in THRESHOLDS:
        far = far + jnp.where(distance >= threshold, 1, 0)
    return jnp.where(distance < 8, distance, far) + jnp.where(relative > 0, 16, 0)


def offset_buckets():
    return jnp.where(
        bucket_of(iota((128, 1024), 1) - 512) == iota((128, 1024), 0), 1.0, 0.0
    ).astype(BF16)


def offset_bias(flat):
    n = BUCKETS * HEADS
    row = jnp.broadcast_to(flat[8:9, :], (16, n))
    h, c = iota((16, n), 0), iota((16, n), 1)
    mine = jnp.where(lax.rem(c, HEADS) == h, row, 0.0).astype(BF16)
    c, b = iota((n, 128), 0), iota((n, 128), 1)
    by_bucket = nn(mine, jnp.where(lax.div(c, HEADS) == b, 1.0, 0.0).astype(BF16))
    return nn(by_bucket.astype(BF16), offset_buckets())


def toeplitz(row):
    wide = jnp.broadcast_to(row, (128, 1024))
    return pltpu.roll(wide, 0, 1, stride=1, stride_axis=0)[:, 128:1024]


def key_span(block):
    return max(0, block - 2) * 128, min(4, block + 3) * 128


def band(i, seg_q, seg_p):
    r, lane = iota((128, 256), 0), iota((128, 256), 1)
    p = 128 * i + 2 * (r & 63) + (r >> 6)
    q = 128 * i - PAD + lane
    same = jnp.concatenate([seg_p, seg_p], axis=0) == seg_q
    one = jnp.where(p == q, 1.0, 0.0)
    two = jnp.where((p >> 1) == (q >> 1), 0.5, 0.0)
    third_p, third_q = (p * 43691) >> 17, (q * 43691) >> 17
    three = jnp.where(same & (third_p == third_q), 1.0, 0.0)
    four = jnp.where(same & ((p >> 2) == (q >> 2)), 1.0, 0.0)
    three = three / jnp.sum(three, axis=1, keepdims=True)
    four = four / jnp.sum(four, axis=1, keepdims=True)
    return one, two, three, four


def band_weights(averages, u):
    scores = [jnp.sum(a * u, axis=1, keepdims=True) for a in averages]
    top = jnp.maximum(jnp.maximum(scores[0], scores[1]), jnp.maximum(scores[2], scores[3]))
    raised = [jnp.exp(s - top) for s in scores]
    total = raised[0] + raised[1] + raised[2] + raised[3]
    return [e / total for e in raised]


def segments(seg_ref, seg_col):
    marked = jnp.broadcast_to(seg_ref[0:1, :].astype(F32) + 1.0, (16, TOK))
    first = jnp.where(iota((16, TOK), 0) == 0, marked, 0.0).astype(BF16)
    seg_col[...] = tn(first, jnp.ones((16, 256), BF16))
    t, j = iota((TOK, SPAN), 0), iota((TOK, SPAN), 1)
    spread = jnp.where(((j - PAD) >> 1) == t, 1.0, 0.0).astype(BF16)
    return nn(marked.astype(BF16), spread)[0:8]


def byte_tables(ids_ref, seg_pad, table):
    ids = jnp.broadcast_to(ids_ref[0:1, :].astype(F32), (8, BYTES))
    ids = pltpu.roll(jnp.concatenate([ids, jnp.zeros((8, 2 * PAD), F32)], axis=1), PAD, 1)
    kept = jnp.full((16, SPAN), -1.0, F32)
    at = iota((16, SPAN), 0)
    for k in range(4):
        turn = (2 - k) % SPAN
        near = ids if turn == 0 else pltpu.roll(ids, turn, 1)
        near_seg = seg_pad if turn == 0 else pltpu.roll(seg_pad, turn, 1)
        row = jnp.where((near_seg == seg_pad) & (seg_pad > 0.5), near, -1.0)
        kept = jnp.where(at == k, jnp.concatenate([row, row], axis=0), kept)
    kept = kept.astype(BF16)
    pick = jnp.where(iota((16, 1024), 0) == (iota((16, 1024), 1) >> 8), 1.0, 0.0).astype(BF16)
    value = (iota((128, 1024), 1) & 255).astype(F32)
    for c in range(SPAN // 128):
        spread = tn(kept[:, 128 * c : 128 * c + 128], pick)
        table[128 * c : 128 * c + 128, :] = jnp.where(spread == value, 1.0, 0.0).astype(BF16)


def tap_table(embed, wide, t_hi, t_low):
    for k in range(4):
        product = embed * wide[k : k + 1, :]
        high = product.astype(BF16)
        t_hi[256 * k : 256 * k + 256, :] = high
        t_low[256 * k : 256 * k + 256, :] = (product - high.astype(F32)).astype(BF16)


def score_row(wide, t_hi, t_low, table):
    score = jnp.broadcast_to(wide[5:6, :], (16, D)).astype(BF16)
    by_tap = nt(score, t_hi[...]) + nt(score, t_low[...])
    u = jnp.sum(nt(split3_rows(by_tap), table[...]), axis=0, keepdims=True)
    return u + jnp.sum(wide[4:5, :] * wide[5:6, :], axis=1, keepdims=True)


def rms_rows(x, gain):
    scale = lax.rsqrt(jnp.mean(x * x, axis=1, keepdims=True) + EPSILON)
    return x * scale * gain


def rms_back(x, gain, dy):
    scale = lax.rsqrt(jnp.mean(x * x, axis=1, keepdims=True) + EPSILON)
    hat = x * scale
    dg = dy * gain
    inner = jnp.mean(dg * hat, axis=1, keepdims=True)
    return scale * (dg - hat * inner), dy * hat


def gelu_parts(x):
    c = 0.7978845608028654
    square = x * x
    t = jnp.tanh(c * x * (1.0 + 0.044715 * square))
    half = 0.5 * (1.0 + t)
    slope = half + 0.5 * x * (1.0 - t * t) * (c * (1.0 + 3 * 0.044715 * square))
    return x * half, slope


def lane_half(e):
    lanes = iota((1, 128), 1)
    return (lanes < 64) if e == 0 else (lanes >= 64)


def masked(x, e):
    return jnp.where(lane_half(e), x, jnp.zeros_like(x))


def forward_mix(seg_col, rows_ref, table, mix):
    @pl.loop(0, BYTES // 128)
    def _(i):
        window = pl.ds(pl.multiple_of(128 * i, 128), 256)
        tokens = pl.ds(pl.multiple_of(64 * i, 64), 64)
        averages = band(i, rows_ref[0:1, window], seg_col[tokens, :])
        weights = band_weights(averages, rows_ref[8:9, window])
        blend = sum(wt * a for wt, a in zip(weights, averages))
        pair = 0.5 * (blend[0:64] + blend[64:128])
        mix[tokens, :] = nn(pair.astype(BF16), table[pl.ds(pl.multiple_of(128 * i, 128), 256), :]).astype(BF16)


def forward_h0(mix, t_hi, wide, h0):
    for c in range(3):
        cols = slice(256 * c, 256 * c + 256)
        h0[:, cols] = nn(mix[...], t_hi[:, cols]) + wide[4:5, cols]


def norm_into(x_ref, gain, out_ref):
    @pl.loop(0, 4)
    def _(i):
        rows = pl.ds(pl.multiple_of(128 * i, 128), 128)
        out_ref[rows, :] = rms_rows(x_ref[rows, :], gain).astype(BF16)


def forward_qkv(w4, attn_in, qkv):
    for n in range(3):
        for c in range(3):
            cols = slice(256 * c, 256 * c + 256)
            qkv[n, :, cols] = nn(attn_in[...], w4[n, :, cols]).astype(BF16)


def forward_pair(hp, qkv, bias_ref, seg_col, rows_tok, probs, ctx):
    lanes = pl.ds(pl.multiple_of(128 * hp, 128), 128)
    keys = qkv[1, :, lanes]
    values = [masked(qkv[2, :, lanes], e) for e in (0, 1)]
    bias = [toeplitz(bias_ref[pl.ds(2 * hp + e, 1), :]) for e in (0, 1)]
    for block in range(4):
        lo, hi = key_span(block)
        rows = slice(128 * block, 128 * block + 128)
        q = qkv[0, rows, lanes]
        seg_p = seg_col[rows, 0:128]
        seg_p = jnp.concatenate([seg_p] * ((hi - lo) // 128), axis=1)
        seen = seg_p == rows_tok[0:1, lo:hi]
        out = jnp.zeros((128, 128), F32)
        for e in (0, 1):
            s = nt(masked(q, e), keys[lo:hi]) * 0.125
            at = (3 - block) * 128 + lo
            s = jnp.where(seen, s + bias[e][:, at : at + hi - lo], -1e9)
            s = jnp.exp(s - jnp.max(s, axis=1, keepdims=True))
            p = (s * (1.0 / jnp.sum(s, axis=1, keepdims=True))).astype(BF16)
            probs[2 * hp + e, rows, lo:hi] = p
            if hi - lo < TOK:
                gap = slice(384, 512) if block == 0 else slice(0, 128)
                probs[2 * hp + e, rows, gap] = jnp.zeros((128, 128), BF16)
            out = out + nn(p, values[e][lo:hi])
        ctx[rows, lanes] = out.astype(BF16)


def forward_out(w4, ctx, h0, h1):
    for c in range(3):
        cols = slice(256 * c, 256 * c + 256)
        h1[:, cols] = h0[:, cols] + nn(ctx[...], w4[3, :, cols])


def forward_ffn(c, wgu, ffn_in, slope_up, gelu, hidden):
    at = pl.multiple_of(256 * c, 256)
    gate = nn(ffn_in[...], wgu[:, pl.ds(at, 256)])
    up = nn(ffn_in[...], wgu[:, pl.ds(pl.multiple_of(FF + at, 256), 256)])
    act, slope = gelu_parts(gate)
    cols = pl.ds(at, 256)
    hidden[:, cols] = (act * up).astype(BF16)
    gelu[:, cols] = act.astype(BF16)
    slope_up[:, cols] = (slope * up).astype(BF16)


def forward_down(wd, hidden, h1, mixed):
    for c in range(3):
        cols = slice(256 * c, 256 * c + 256)
        mixed[:, cols] = (h1[:, cols] + nn(hidden[...], wd[:, cols])).astype(BF16)


def backward_hidden(c, wd, dl, hidden, slope_up, gelu, dgate, dup, gd):
    cols = pl.ds(pl.multiple_of(256 * c, 256), 256)
    dh = nt(dl[...], wd[cols, :])
    dgate[:, cols] = (dh * slope_up[:, cols].astype(F32)).astype(BF16)
    dup[:, cols] = (dh * gelu[:, cols].astype(F32)).astype(BF16)
    gd[cols, :] = tn(hidden[:, cols], dl[...]).astype(BF16)


def backward_gate_up(c, ffn_in, dgate, dup, ggu):
    at = pl.multiple_of(256 * c, 256)
    cols = pl.ds(at, 256)
    ggu[:, cols] = tn(ffn_in[...], dgate[:, cols]).astype(BF16)
    ggu[:, pl.ds(pl.multiple_of(FF + at, 256), 256)] = tn(ffn_in[...], dup[:, cols]).astype(BF16)


def backward_ffn_in(wgu, dgate, dup, dx):
    for c in range(3):
        rows = slice(256 * c, 256 * c + 256)
        dx[:, rows] = nt(dgate[...], wgu[rows, 0:FF]) + nt(dup[...], wgu[rows, FF:])


def backward_norm(x_ref, gain, dy_ref, add, out_ref):
    def step(i, total):
        rows = pl.ds(pl.multiple_of(128 * i, 128), 128)
        dx, dgain = rms_back(x_ref[rows, :], gain, dy_ref[rows, :])
        out_ref[rows, :] = add[rows, :].astype(F32) + dx
        return total + jnp.sum(dgain, axis=0, keepdims=True)

    return lax.fori_loop(0, 4, step, jnp.zeros((1, D), F32))


def backward_out(w4, ctx, dh1, da, dctx, g4):
    da[...] = dh1[...].astype(BF16)
    for c in range(3):
        cols = slice(256 * c, 256 * c + 256)
        dctx[:, cols] = nt(da[...], w4[3, cols, :]).astype(BF16)
        g4[3, :, cols] = tn(ctx[...], da[:, cols]).astype(BF16)


def diagonal_sums(x):
    total = x[0:8, :]
    for a in range(1, 16):
        total = total + pltpu.roll(x[8 * a : 8 * a + 8, :], 1024 - 8 * a, 1)
    row = iota((8, 1024), 0)
    for bit in (1, 2, 4):
        total = jnp.where((row & bit) != 0, pltpu.roll(total, 1024 - bit, 1), total)
    return jnp.sum(total, axis=0, keepdims=True)


def backward_pair(hp, qkv, probs, ctx, dctx, dqkv, by_offset, ds_ref, bias_sum):
    lanes = pl.ds(pl.multiple_of(128 * hp, 128), 128)
    q, keys, values = (qkv[n, :, lanes] for n in range(3))
    dc = dctx[:, lanes]
    inner = dc.astype(F32) * ctx[:, lanes].astype(F32)
    dk = jnp.zeros((TOK, 128), F32)
    dv = jnp.zeros((TOK, 128), F32)
    for e in (0, 1):
        p_ref = probs.at[e]
        bias_sum[...] = jnp.zeros_like(bias_sum)
        for block in range(4):
            lo, hi = key_span(block)
            rows = slice(128 * block, 128 * block + 128)
            delta = jnp.sum(masked(inner[rows], e), axis=1, keepdims=True)
            dp = nt(masked(dc[rows], e), values[lo:hi])
            ds = p_ref[rows, lo:hi].astype(F32) * (dp - delta)
            at = (3 - block) * 128 + lo
            bias_sum[:, at : at + hi - lo] += ds
            ds_ref[e, rows, lo:hi] = ds.astype(BF16)
            if hi - lo < TOK:
                gap = slice(384, 512) if block == 0 else slice(0, 128)
                ds_ref[e, rows, gap] = jnp.zeros((128, 128), BF16)
        dv = dv + tn(p_ref[...], masked(dc, e))
        dk = dk + tn(ds_ref[e], masked(q, e))
        by_offset[pl.ds(2 * hp + e, 1), :] = diagonal_sums(bias_sum)
    dq = jnp.concatenate(
        [
            nn(ds_ref[0, 128 * b : 128 * b + 128, :], masked(keys, 0))
            + nn(ds_ref[1, 128 * b : 128 * b + 128, :], masked(keys, 1))
            for b in range(4)
        ],
        axis=0,
    )
    dqkv[0, :, lanes] = (dq * 0.125).astype(BF16)
    dqkv[1, :, lanes] = (dk * 0.125).astype(BF16)
    dqkv[2, :, lanes] = dv.astype(BF16)


def bias_gradient(by_offset):
    buckets = bucket_of(iota((128, 1024), 1) - 384)
    pick = jnp.where(buckets == iota((128, 1024), 0), 1.0, 0.0).astype(BF16)
    total = jnp.zeros((16, 128), F32)
    rest = by_offset
    for _ in range(3):
        part = rest.astype(BF16)
        total = total + nt(part, pick)
        rest = rest - part.astype(F32)
    n = BUCKETS * HEADS
    b, c = iota((128, n), 0), iota((128, n), 1)
    place = jnp.where(lax.div(c, HEADS) == b, 1.0, 0.0).astype(BF16)
    spread = jnp.zeros((16, n), F32)
    rest = total
    for _ in range(3):
        part = rest.astype(BF16)
        spread = spread + nn(part, place)
        rest = rest - part.astype(F32)
    h, c = iota((16, n), 0), iota((16, n), 1)
    return jnp.sum(jnp.where(lax.rem(c, HEADS) == h, spread, 0.0), axis=0, keepdims=True)


def backward_qkv(w4, attn_in, dqkv, dx, g4):
    for c in range(3):
        cols = slice(256 * c, 256 * c + 256)
        total = jnp.zeros((TOK, 256), F32)
        for n in range(3):
            total = total + nt(dqkv[n], w4[n, cols, :])
            g4[n, :, cols] = tn(attn_in[...], dqkv[n, :, cols]).astype(BF16)
        dx[:, cols] = total


def backward_gbst(we, wide, seg_col, rows_ref, table, t_hi, t_low, mix, dh0, dh0_low, q_ref, du_ref, dt_ref, ge):
    dh0_low[...] = dh0[...].astype(BF16)
    for c in range(4):
        rows = slice(256 * c, 256 * c + 256)
        q_ref[:, rows] = nt(dh0_low[...], t_hi[rows, :]).astype(BF16)
    du_ref[...] = jnp.zeros_like(du_ref)

    @pl.loop(0, BYTES // 128)
    def _(i):
        window = pl.ds(pl.multiple_of(128 * i, 128), 256)
        tokens = pl.ds(pl.multiple_of(64 * i, 64), 64)
        averages = band(i, rows_ref[0:1, window], seg_col[tokens, :])
        weights = band_weights(averages, rows_ref[8:9, window])
        near = nt(q_ref[tokens, :], table[pl.ds(pl.multiple_of(128 * i, 128), 256), :])
        near = near + jnp.sum(dh0[tokens, :] * wide[4:5, :], axis=1, keepdims=True)
        near = jnp.concatenate([near, near], axis=0) * 0.5
        dws = [jnp.sum(a * near, axis=1, keepdims=True) for a in averages]
        mean = sum(wt * dw for wt, dw in zip(weights, dws))
        total = sum((wt * (dw - mean)) * a for wt, dw, a in zip(weights, dws, averages))
        du_ref[0:1, window] += jnp.sum(total, axis=0, keepdims=True)

    du = du_ref[0:1, :]
    du_sum = jnp.sum(du, axis=1, keepdims=True)
    by_tap = jnp.sum(nn(split3_rows(jnp.broadcast_to(du, (16, SPAN))), table[...]), axis=0, keepdims=True)
    parts = split3_rows(jnp.broadcast_to(by_tap, (16, 1024)))
    score = jnp.broadcast_to(wide[5:6, :], (16, D)).astype(BF16)
    for c in range(4):
        rows = slice(256 * c, 256 * c + 256)
        dt_ref[rows, :] = tn(mix[:, rows], dh0_low[...]) + tn(parts[:, rows], score)
    dscore = jnp.sum(nn(parts, t_hi[...]) + nn(parts, t_low[...]), axis=0, keepdims=True) + du_sum * wide[4:5, :]
    dconv_b = jnp.sum(dh0[...], axis=0, keepdims=True) + du_sum * wide[5:6, :]
    embed = we[...].astype(F32)
    dconv = []
    dembed = jnp.zeros((VOCAB, D), F32)
    for k in range(4):
        dt = dt_ref[256 * k : 256 * k + 256, :]
        dembed = dembed + dt * wide[k : k + 1, :]
        dconv.append(jnp.sum(dt * embed, axis=0, keepdims=True))
    ge[...] = dembed.astype(BF16)
    return dconv, dconv_b, dscore


def pack_smalls(sz, rows, flat, out):
    at = iota((16, D), 0)
    wide = jnp.zeros((16, D), F32)
    for n, row in enumerate(rows):
        wide = jnp.where(at == n, jnp.broadcast_to(row, (16, D)), wide)
    wide = wide.astype(BF16)
    n = BUCKETS * HEADS
    rel = jnp.where(iota((16, n), 0) == 8, jnp.broadcast_to(flat, (16, n)), 0.0).astype(BF16)
    for s in range(sz.shards):
        c, i = iota((D, 128), 0), iota((D, 128), 1)
        place = jnp.where((c == i + s * sz.d) & (i < sz.d), 1.0, 0.0).astype(BF16)
        c, i = iota((n, 128), 0), iota((n, 128), 1)
        place_rel = jnp.where((c == i + s * sz.rel) & (i < sz.rel), 1.0, 0.0).astype(BF16)
        out[s] = (nn(wide, place) + nn(rel, place_rel)).astype(BF16)


class Place:
    def __init__(self, shards, copies):
        self.shards, self.copies = shards, copies
        self.inner = 2 if shards < 16 else 4
        self.outer = shards // self.inner
        self.planes = copies // 2
        f, d = lax.axis_index("fsdp"), lax.axis_index("dp")
        self.f, self.d = f, d
        self.f1, self.f2 = lax.div(f, self.inner), lax.rem(f, self.inner)
        self.x, self.core = lax.div(d, 2), lax.rem(d, 2)

    def shard(self, k, i):
        f1 = lax.rem(self.f1 + (self.outer - k), self.outer)
        f2 = lax.rem(self.f2 + (self.inner - i), self.inner)
        return f1 * self.inner + f2

    def outer_peer(self, k):
        return (lax.rem(self.f1 + k, self.outer) * self.inner + self.f2, self.d)

    def inner_peer(self, i):
        return (self.f1 * self.inner + lax.rem(self.f2 + i, self.inner), self.d)

    def plane_peer(self, p):
        return (self.f, lax.rem(self.x + p, self.planes) * 2 + self.core)

    def sibling(self):
        return (self.f, self.x * 2 + (1 - self.core))

    def barrier(self):
        peers = [self.outer_peer(k) for k in range(1, self.outer)]
        peers += [self.inner_peer(i) for i in range(1, self.inner)]
        peers += [self.plane_peer(p) for p in range(1, self.planes)]
        peers += [self.sibling()]
        sem = pltpu.get_barrier_semaphore()
        for peer in peers:
            pl.semaphore_signal(sem, inc=1, device_id=peer, device_id_type=MESH)
        pl.semaphore_wait(sem, len(peers))


def aligned(value, unit):
    return value if isinstance(value, int) else pl.multiple_of(value, unit)


def remote(src, dst, send, recv, peer):
    return pltpu.make_async_remote_copy(
        src_ref=src, dst_ref=dst, send_sem=send, recv_sem=recv, device_id=peer, device_id_type=MESH
    )


class Part:
    def __init__(self, stride, first, rows, base, gap, half, lone):
        self.stride, self.first, self.rows = stride, first, rows
        self.base, self.gap, self.half, self.lone = base, gap, half, lone

    def split(self, place):
        return self.lone if place.planes == 2 else 0

    def wide(self, place):
        return self.half - self.split(place)

    def row(self, shard):
        return aligned(shard * self.stride + self.first, 16)

    def view(self, ref, shard, column, width):
        return ref.at[pl.ds(self.row(shard), self.rows), pl.ds(aligned(column, 128), width)]

    def start(self, place):
        return place.core * self.gap + self.base

    def mine(self, ref, place, shard):
        return self.view(ref, shard, self.start(place) + place.x * self.split(place), self.wide(place))

    def kept(self, ref, place, shard):
        return self.view(ref, shard, self.start(place) + place.x * self.wide(place), self.lone)

    def lacked(self, ref, place, shard):
        return self.view(ref, shard, self.start(place) + (1 - place.x) * self.wide(place), self.lone)


class Gather:
    @staticmethod
    def copies(shards, planes_split=True):
        return shards * 2 + 8 + shards

    def __init__(self, place, part, ref, send, recv, all_rows):
        self.place, self.part, self.ref = place, part, ref
        self.send, self.recv = send, recv
        self.all_rows = all_rows
        self.sent = []

    def _slot(self, kind, k=0, i=0):
        n = self.place.shards
        return {"o": k, "i": n + k * self.place.inner + i, "p": 2 * n + k * self.place.inner + i, "c": 3 * n}[kind]

    def _start(self, kind, view, peer, k=0, i=0):
        n = self._slot(kind, k, i)

        def make():
            here = view()
            return remote(here, here, self.send.at[n], self.recv.at[n], peer())

        make().start()
        self.sent.append(make)

    def _await(self, kind, view, peer, k=0, i=0):
        n = self._slot(kind, k, i)
        remote(view, view, self.send.at[n], self.recv.at[n], peer).wait_recv()

    def _plane(self, k, i):
        place = self.place
        if self.part.split(place):
            self._start(
                "p", lambda: self.part.kept(self.ref, place, place.shard(k, i)), lambda: place.plane_peer(1), k, i
            )

    def first(self):
        place = self.place

        def own():
            return self.part.mine(self.ref, place, place.f)

        for k in range(1, place.outer):
            self._start("o", own, functools.partial(place.outer_peer, k), k)
        for i in range(1, place.inner):
            self._start("i", own, functools.partial(place.inner_peer, i), 0, i)

    def second(self):
        place = self.place
        for k in range(1, place.outer):

            def view(k=k):
                return self.part.mine(self.ref, place, place.shard(k, 0))

            self._await("o", view(), place.outer_peer(k), k)
            for i in range(1, place.inner):
                self._start("i", view, functools.partial(place.inner_peer, i), k, i)
            self._plane(k, 0)

    def third(self):
        place = self.place
        for k in range(place.outer):
            for i in range(1, place.inner):
                view = self.part.mine(self.ref, place, place.shard(k, i))
                self._await("i", view, place.inner_peer(i), k, i)
                self._plane(k, i)

    def _half(self, core):
        part = self.part
        column = core * part.gap + part.base
        if part.rows == part.stride:
            return self.ref.at[:, pl.ds(aligned(column, 128), part.half)]
        return None

    def fourth(self):
        place, part = self.place, self.part
        if part.split(place):
            for k, i in [(k, i) for k in range(place.outer) for i in range(place.inner) if k or i]:
                view = part.lacked(self.ref, place, place.shard(k, i))
                self._await("p", view, place.plane_peer(1), k, i)
        n = self._slot("c")
        for s in range(place.shards if part.rows != part.stride else 1):

            def make(s=s):
                view = self._half(place.core)
                if view is None:
                    view = part.view(self.ref, s, part.start(place), part.half)
                return remote(view, view, self.send.at[n + s], self.recv.at[n + s], place.sibling())

            make().start()
            self.sent.append(make)

    def fifth(self):
        place, part = self.place, self.part
        n = self._slot("c")
        for s in range(place.shards if part.rows != part.stride else 1):
            view = self._half(1 - place.core)
            if view is None:
                view = part.view(self.ref, s, (1 - place.core) * part.gap + part.base, part.half)
            remote(view, view, self.send.at[n + s], self.recv.at[n + s], place.sibling()).wait_recv()

    def finish(self):
        for make in self.sent:
            make().wait_send()


def add_rows(target, source, rows, step):
    if rows <= step:
        target[...] = (target[...].astype(F32) + source[...].astype(F32)).astype(BF16)
        return

    @pl.loop(0, rows // step)
    def _(n):
        at = pl.ds(pl.multiple_of(n * step, step), step)
        target[at, :] = (target[at, :].astype(F32) + source[at, :].astype(F32)).astype(BF16)


class Reduce:
    @staticmethod
    def buffers(shards, copies, part):
        inner = 2 if shards < 16 else 4
        outer = shards // inner
        planes = copies // 2
        split = part.lone if planes == 2 else 0
        wide = part.half - split
        shapes = [
            (shards * part.stride, part.half),
            (shards * part.stride, split) if split else (16, 128),
            (inner - 1, outer, part.rows, wide),
            (outer - 1, part.rows, wide),
            (planes - 1, part.rows, wide),
            (part.rows, part.half),
            (part.rows, part.half),
        ]
        return [pltpu.VMEM(s, BF16) for s in shapes]

    @staticmethod
    def sems(shards, copies):
        return 2 + 2 * shards + copies + 2

    def __init__(self, place, part, ref, bufs, send, recv):
        self.place, self.part, self.ref = place, part, ref
        self.from_core, self.from_plane, self.from_inner, self.from_outer, self.last, self.whole, self.other = bufs
        self.send, self.recv = send, recv
        self.sent = []
        self.rows = place.shards * part.stride

    def _start(self, n, src, dst, peer):
        def make():
            return remote(src(), dst(), self.send.at[n], self.recv.at[n], peer())

        make().start()
        self.sent.append(make)

    def _await(self, n, dst, peer):
        remote(dst, dst, self.send.at[n], self.recv.at[n], peer).wait_recv()

    def _columns(self, column, width):
        return self.ref.at[:, pl.ds(aligned(column, 128), width)]

    def first(self):
        place, part = self.place, self.part
        self._start(
            0,
            lambda: self._columns((1 - place.core) * part.gap + part.base, part.half),
            lambda: self.from_core,
            place.sibling,
        )

    def second(self):
        place, part = self.place, self.part
        self._await(0, self.from_core, place.sibling())
        target = self._columns(part.start(place), part.half)
        add_rows(target, self.from_core, self.rows, 64)
        if part.split(place):
            self._start(
                1,
                lambda: self._columns(part.start(place) + (1 - place.x) * part.wide(place), part.lone),
                lambda: self.from_plane,
                functools.partial(place.plane_peer, 1),
            )
        else:
            self._inner()

    def _inner(self):
        place, part = self.place, self.part
        for i in range(1, place.inner):
            for k in range(place.outer):

                def src(i=i, k=k):
                    f1 = lax.rem(place.f1 + k, place.outer)
                    f2 = lax.rem(place.f2 + i, place.inner)
                    return part.mine(self.ref, place, f1 * place.inner + f2)

                self._start(
                    2 + i * place.outer + k,
                    src,
                    functools.partial(lambda i, k: self.from_inner.at[i - 1, k], i, k),
                    functools.partial(place.inner_peer, i),
                )

    def third(self):
        place, part = self.place, self.part
        if part.split(place):
            self._await(1, self.from_plane, place.plane_peer(1))
            target = self._columns(part.start(place) + place.x * part.wide(place), part.lone)
            add_rows(target, self.from_plane, self.rows, 128)
            self._inner()

    def fourth(self):
        place, part = self.place, self.part
        for i in range(1, place.inner):
            for k in range(place.outer):
                self._await(2 + i * place.outer + k, self.from_inner.at[i - 1, k], place.inner_peer(i))
        for k in list(range(1, place.outer)) + [0]:

            def mine(k=k):
                f1 = lax.rem(place.f1 + k, place.outer)
                return part.mine(self.ref, place, f1 * place.inner + place.f2)

            target = mine()
            total = target[...].astype(F32)
            for i in range(1, place.inner):
                total = total + self.from_inner[i - 1, k].astype(F32)
            target[...] = total.astype(BF16)
            if k:
                self._start(
                    2 + place.shards + k,
                    mine,
                    functools.partial(lambda k: self.from_outer.at[k - 1], k),
                    functools.partial(place.outer_peer, k),
                )

    def fifth(self):
        place, part = self.place, self.part
        for k in range(1, place.outer):
            self._await(2 + place.shards + k, self.from_outer.at[k - 1], place.outer_peer(k))
        target = part.mine(self.ref, place, place.f)
        total = target[...].astype(F32)
        for k in range(1, place.outer):
            total = total + self.from_outer[k - 1].astype(F32)
        target[...] = total.astype(BF16)
        for p in range(1, place.planes):
            self._start(
                2 + 2 * place.shards + p,
                lambda: part.mine(self.ref, place, place.f),
                functools.partial(lambda p: self.last.at[p - 1], p),
                functools.partial(place.plane_peer, p),
            )

    def sixth(self):
        place, part = self.place, self.part
        for p in range(1, place.planes):
            self._await(2 + 2 * place.shards + p, self.last.at[p - 1], place.plane_peer(p))
        mine = part.mine(self.ref, place, place.f)[...].astype(F32)
        if part.split(place):
            theirs = self.last[0].astype(F32)
            lone, wide, both = part.lone, part.wide(place), part.half - 2 * part.lone
            low = place.x == 0
            if both:
                shared = jnp.where(low, mine[:, lone:], mine[:, :both]) + jnp.where(low, theirs[:, :both], theirs[:, lone:])
                self.whole[:, lone:wide] = shared.astype(BF16)
            self.whole[:, 0:lone] = jnp.where(low, mine[:, 0:lone], theirs[:, 0:lone]).astype(BF16)
            self.whole[:, wide:] = jnp.where(low, theirs[:, both:], mine[:, both:]).astype(BF16)
        else:
            for p in range(1, place.planes):
                mine = mine + self.last[p - 1].astype(F32)
            self.whole[...] = mine.astype(BF16)
        n = 2 + 2 * place.shards + place.copies
        self._start(n, lambda: self.whole, lambda: self.other, place.sibling)

    def seventh(self, out):
        place = self.place
        self._await(2 + 2 * place.shards + place.copies, self.other, place.sibling())
        mine, theirs = self.whole[...].astype(F32), self.other[...].astype(F32)
        low = place.core == 0
        out(0, jnp.where(low, mine, theirs))
        out(1, jnp.where(low, theirs, mine))

    def finish(self):
        for make in self.sent:
            make().wait_send()


VMEM_LIMIT = 64 * 1024 * 1024 - 65536


def shape(dims, dtype):
    return jax.ShapeDtypeStruct(dims, dtype)


def in_vmem(s):
    return pltpu.VMEM(s.shape, s.dtype)


def saved_shapes():
    return dict(
        mixed=shape((TOK, D), BF16),
        attn_in=shape((TOK, D), BF16),
        qkv=shape((3, TOK, D), BF16),
        probs=shape((HEADS, TOK, TOK), BF16),
        ctx=shape((TOK, D), BF16),
        h0=shape((TOK, D), F32),
        h1=shape((TOK, D), F32),
        ffn_in=shape((TOK, D), BF16),
        slope_up=shape((TOK, FF), BF16),
        gelu=shape((TOK, FF), BF16),
        hidden=shape((TOK, FF), BF16),
        table=shape((SPAN, 1024), BF16),
        t_hi=shape((1024, D), BF16),
        t_low=shape((1024, D), BF16),
        mix=shape((TOK, 1024), BF16),
        rows_ref=shape((16, SPAN), F32),
        seg_col=shape((TOK, 256), F32),
        wide_ref=shape((16, D), F32),
        we=shape((VOCAB, D), BF16),
        w4=shape((4, D, D), BF16),
        wgu=shape((D, 2 * FF), BF16),
        wd=shape((FF, D), BF16),
    )


SAVED = tuple(saved_shapes())


def gather_parts(sz):
    parts = [("we", None, Part(sz.emb, 0, sz.emb, 0, 384, 384, 0))]
    parts += [("w4", n, Part(sz.d, 0, sz.d, 0, 384, 384, 128)) for n in range(4)]
    for j, lone in enumerate((128, 256, 128, 128)):
        parts.append(("wgu", None, Part(sz.d, 0, sz.d, 512 * j, FF, 512, lone)))
    for j in range(2):
        parts.append(("wd", None, Part(sz.ff, j * sz.ff // 2, sz.ff // 2, 0, 384, 384, 128)))
    return parts


def forward_kernel(sz, copies, *refs):
    (ids, seg, embed, conv_w, conv_b, score_w, norm_attn, w_q, w_k, w_v, w_o, rel, norm_ffn, w_g, w_u, w_d) = refs[:16]
    outs = dict(zip(SAVED, refs[16 : 16 + len(SAVED)]))
    refs = refs[16 + len(SAVED) :]
    r = dict(zip(SAVED, refs[: len(SAVED)]))
    small, stage, bias_ref, out_sems, send, recv, small_send, small_recv = refs[len(SAVED) :]
    place = Place(sz.shards, copies)
    started = []

    def save(*names):
        for name in names:
            copy = pltpu.make_async_copy(r[name], outs[name], out_sems.at[SAVED.index(name)])
            copy.start()
            started.append(copy)

    jobs = []
    for n, (name, lead, part) in enumerate(gather_parts(sz)):
        ref = r[name] if lead is None else r[name].at[lead]
        jobs.append(Gather(place, part, ref, send.at[n], recv.at[n], None))
    acts = {"Z": Gather.first, "Y": Gather.second, "X": Gather.third, "C": Gather.fourth, "W": Gather.fifth}

    def go(*words):
        for word in words:
            acts[word[0]](jobs[int(word[1:])])

    f = place.f

    def own(rows):
        return pl.ds(pl.multiple_of(f * rows, 16), rows)

    small_started = []

    def small_copy(k, i, peer):
        n = k * place.inner + i
        tile = small.at[place.shard(k, 0)] if i else small.at[f]
        copy = remote(tile, tile, small_send.at[n], small_recv.at[n], peer)
        copy.start()
        small_started.append(copy)

    def small_await(k, i, peer):
        n = k * place.inner + i
        tile = small.at[place.shard(k, i)]
        remote(tile, tile, small_send.at[n], small_recv.at[n], peer).wait_recv()

    stage[...] = jnp.zeros_like(stage)
    stage[0:4, 0 : sz.d] = conv_w[...]
    for n, row in enumerate((conv_b, score_w, norm_attn, norm_ffn)):
        stage[4 + n : 5 + n, 0 : sz.d] = row[...].reshape(1, sz.d)
    stage[8:9, 0 : sz.rel] = rel[...].reshape(1, sz.rel)
    small[f] = stage[...].astype(BF16)
    mine = pl.ds(pl.multiple_of(place.core * 384, 128), 384)
    r["we"][own(sz.emb), mine] = embed[:, mine].astype(BF16)
    place.barrier()
    for k in range(1, place.outer):
        small_copy(k, 0, place.outer_peer(k))
    for i in range(1, place.inner):
        small_copy(0, i, place.inner_peer(i))
    go("Z0")
    for n, w in enumerate((w_q, w_k, w_v, w_o)):
        r["w4"][n, own(sz.d), mine] = w[:, mine].astype(BF16)
    go("Z1", "Z2", "Z3")
    @pl.when(place.core == 0)
    def _():
        r["wgu"][own(sz.d), 0:FF] = w_g[...].astype(BF16)

    @pl.when(place.core == 1)
    def _():
        r["wgu"][own(sz.d), FF:] = w_u[...].astype(BF16)

    r["wd"][own(sz.ff), mine] = w_d[:, mine].astype(BF16)

    seg_pad = segments(seg, r["seg_col"])
    for k in range(1, place.outer):
        small_await(k, 0, place.outer_peer(k))
        for i in range(1, place.inner):
            small_copy(k, i, place.inner_peer(i))
    go("Y0")
    byte_tables(ids, seg_pad, r["table"])
    save("table", "seg_col")
    go("X0", "C0")
    for k in range(place.outer):
        for i in range(1, place.inner):
            small_await(k, i, place.inner_peer(i))
    wide, flat = expand_smalls(sz, small)
    r["wide_ref"][...] = wide
    bias_ref[...] = offset_bias(flat)
    go("W0", "Z4", "Y1", "Y2", "Y3")
    save("we", "wide_ref")
    tap_table(r["we"][...].astype(F32), wide, r["t_hi"], r["t_low"])
    r["rows_ref"][0:8, :] = seg_pad
    r["rows_ref"][8:16, :] = jnp.broadcast_to(score_row(wide, r["t_hi"], r["t_low"], r["table"]), (8, SPAN))
    save("t_hi", "t_low", "rows_ref")
    go("Z5", "Z6", "X1", "X2", "X3", "Y4")
    forward_mix(r["seg_col"], r["rows_ref"], r["table"], r["mix"])
    save("mix")
    go("Z7", "C1", "C2", "C3", "X4", "Y5")
    forward_h0(r["mix"], r["t_hi"], wide, r["h0"])
    save("h0")
    norm_into(r["h0"], r["wide_ref"][6:7, :], r["attn_in"])
    save("attn_in")
    go("W1", "W2", "W3")
    forward_qkv(r["w4"], r["attn_in"], r["qkv"])
    save("qkv")
    go("Z8", "C4", "X5", "Y6")
    rows_tok = seg[0:1, :].astype(F32) + 1.0

    @pl.loop(0, 6)
    def _(hp):
        forward_pair(hp, r["qkv"], bias_ref, r["seg_col"], rows_tok, r["probs"], r["ctx"])

        @pl.when(hp == 1)
        def _():
            go("Z9", "C5", "X6", "Y7")

        @pl.when(hp == 3)
        def _():
            go("Z10", "C6", "X7", "Y8")

    save("probs", "ctx")
    go("W4", "C7", "X8", "Y9")
    save("w4")
    forward_out(r["w4"], r["ctx"], r["h0"], r["h1"])
    save("h1")
    norm_into(r["h1"], r["wide_ref"][7:8, :], r["ffn_in"])
    save("ffn_in")
    for j, words in enumerate((("W5",), ("W6",), ("W7", "C8", "X9", "Y10"), ("W8", "C9", "X10"))):
        go(*words)

        @pl.loop(2 * j, 2 * j + 2)
        def _(c):
            forward_ffn(c, r["wgu"], r["ffn_in"], r["slope_up"], r["gelu"], r["hidden"])

    save("wgu", "slope_up", "gelu", "hidden")
    go("C10", "W9", "W10")
    save("wd")
    forward_down(r["wd"], r["hidden"], r["h1"], r["mixed"])
    save("mixed")
    for job in jobs:
        job.finish()
    for copy in small_started:
        copy.wait_send()
    for copy in started:
        copy.wait()


def reduce_parts(sz):
    parts = [("gd", None, Part(sz.ff, 0, sz.ff, 0, 384, 384, 128))]
    for j, lone in enumerate((128, 256, 128, 128)):
        parts.append(("ggu", None, Part(sz.d, 0, sz.d, 512 * j, FF, 512, lone)))
    parts += [("g4", n, Part(sz.d, 0, sz.d, 0, 384, 384, 128)) for n in (3, 2, 0, 1)]
    parts.append(("ge", None, Part(sz.emb, 0, sz.emb, 0, 384, 384, 0)))
    return parts


def load(sems, pairs):
    found = [pltpu.make_async_copy(s, d, sems.at[n]) for n, (s, d) in enumerate(pairs)]
    for copy in found:
        copy.start()
    return found


BACK_IN = tuple(name for name in SAVED if name != "mixed")


def backward_kernel(sz, copies, *refs):
    n_in = 1 + len(BACK_IN)
    dl_h = refs[0]
    h = dict(zip(BACK_IN, refs[1:n_in]))
    o_e, o_cw, o_cb, o_sw, o_na, o_q, o_k, o_v, o_o, o_rel, o_nf, o_g, o_u, o_d = refs[n_in : n_in + 14]
    refs = refs[n_in + 14 :]
    ge, g4, ggu, gd, gs, dl, wide_ref, h1, ctx, dx, dh1, by_off, sems, send, recv = refs[:15]
    small_other, small_inner, small_outer, small_last, small_send, small_recv = refs[15:21]
    buffers = refs[21:]
    place = Place(sz.shards, copies)
    grads = dict(ge=ge, g4=g4, ggu=ggu, gd=gd)
    jobs = []
    for n, (name, lead, part) in enumerate(reduce_parts(sz)):
        ref = grads[name] if lead is None else grads[name].at[lead]
        jobs.append(Reduce(place, part, ref, buffers[7 * n : 7 * n + 7], send.at[n], recv.at[n]))

    def half(ref):
        def write(core, values):
            ref[:, 384 * core : 384 * core + 384] = values

        return write

    def gate_up(j):
        def write(core, values):
            (o_g, o_u)[core][:, 512 * j : 512 * j + 512] = values

        return write

    writers = [half(o_d)] + [gate_up(j) for j in range(4)] + [half(x) for x in (o_o, o_v, o_q, o_k, o_e)]
    acts = {
        "C": Reduce.first,
        "X": Reduce.second,
        "Y": Reduce.third,
        "Z": Reduce.fourth,
        "L": Reduce.fifth,
        "S": Reduce.sixth,
    }

    def go(*words):
        for word in words:
            n = int(word[1:])
            if word[0] == "W":
                jobs[n].seventh(writers[n])
            else:
                acts[word[0]](jobs[n])

    pre = load(sems.at[0], [(dl_h, dl), (h["wide_ref"], wide_ref), (h["h1"], h1), (h["ctx"], ctx)])

    def phase1(wd, hidden, slope, gelu, wgu, ffn_in):
        names = ("wd", "slope_up", "gelu", "hidden", "wgu", "ffn_in")
        a = load(sems.at[1], [(h[n], d) for n, d in zip(names, (wd, slope, gelu, hidden, wgu, ffn_in))])
        place.barrier()
        for copy in a[:4] + pre:
            copy.wait()

        @pl.loop(0, 8)
        def _(c):
            backward_hidden(c, wd, dl, hidden, slope, gelu, slope, gelu, gd)

        go("C0")
        for copy in a[4:]:
            copy.wait()
        backward_ffn_in(wgu, slope, gelu, dx)
        for j, words in enumerate((("C1", "X0"), ("C2", "X1", "Y0"), ("C3", "X2", "Y1", "Z0"), ("C4", "X3", "Y2", "Z1", "L0"))):
            @pl.loop(2 * j, 2 * j + 2)
            def _(c):
                backward_gate_up(c, ffn_in, slope, gelu, ggu)

            go(*words)

    pl.run_scoped(
        phase1,
        pltpu.VMEM((FF, D), BF16),
        pltpu.VMEM((TOK, FF), BF16),
        pltpu.VMEM((TOK, FF), BF16),
        pltpu.VMEM((TOK, FF), BF16),
        pltpu.VMEM((D, 2 * FF), BF16),
        pltpu.VMEM((TOK, D), BF16),
    )
    dnorm_ffn = backward_norm(h1, wide_ref[7:8, :], dx, dl, dh1)

    def phase2(w4, qkv, probs, da, dctx, ds_ref, bias_sum, attn_in, psem):
        a = load(sems.at[2], [(h["w4"], w4), (h["qkv"], qkv), (h["attn_in"], attn_in)])

        def fetch(hp, slot):
            return pltpu.make_async_copy(h["probs"].at[pl.ds(2 * hp, 2)], probs.at[slot], psem.at[slot])

        fetch(0, 0).start()
        a[0].wait()
        backward_out(w4, ctx, dh1, da, dctx, g4)
        go("C5", "X4", "Y3", "Z2", "L1", "S0")
        by_off[...] = jnp.zeros_like(by_off)
        bias_sum[...] = jnp.zeros_like(bias_sum)
        a[1].wait()

        @pl.loop(0, 6)
        def _(hp):
            slot = lax.rem(hp, 2)

            @pl.when(hp < 5)
            def _():
                fetch(hp + 1, 1 - slot).start()

            fetch(hp, slot).wait()
            backward_pair(hp, qkv, probs.at[slot], ctx, dctx, qkv, by_off, ds_ref, bias_sum)

            @pl.when(hp == 1)
            def _():
                go("X5", "Y4", "Z3", "L2", "S1", "W0")

            @pl.when(hp == 3)
            def _():
                go("Y5", "Z4", "L3", "S2", "W1")

        a[2].wait()
        backward_qkv(w4, attn_in, qkv, dx, g4)
        go("C6", "C7", "C8", "Z5", "L4", "S3", "W2")

    pl.run_scoped(
        phase2,
        pltpu.VMEM((4, D, D), BF16),
        pltpu.VMEM((3, TOK, D), BF16),
        pltpu.VMEM((2, 2, TOK, TOK), BF16),
        pltpu.VMEM((TOK, D), BF16),
        pltpu.VMEM((TOK, D), BF16),
        pltpu.VMEM((2, TOK, TOK), BF16),
        pltpu.VMEM((128, 1024), F32),
        pltpu.VMEM((TOK, D), BF16),
        pltpu.SemaphoreType.DMA((2,)),
    )

    def phase3(we, h0, rows_ref, seg_col, table, t_hi, t_low, mix, da, dt_ref, q_ref, du_ref):
        names = ("h0", "we", "rows_ref", "seg_col", "table", "t_hi", "t_low", "mix")
        a = load(sems.at[3], [(h[n], d) for n, d in zip(names, (h0, we, rows_ref, seg_col, table, t_hi, t_low, mix))])
        a[0].wait()
        go("X6", "X7", "X8")
        dnorm_attn = backward_norm(h0, wide_ref[6:7, :], dx, dh1, dx)
        wide = wide_ref[...]
        for copy in a[1:]:
            copy.wait()
        go("Y6", "Y7", "Y8", "L5", "S4", "W3")
        dconv, dconv_b, dscore = backward_gbst(
            we, wide, seg_col, rows_ref, table, t_hi, t_low, mix, dx, da, q_ref, du_ref, dt_ref, ge
        )
        go("C9", "Z6", "Z7", "Z8")
        pack_smalls(sz, dconv + [dconv_b, dscore, dnorm_attn, dnorm_ffn], bias_gradient(by_off[...]), gs)

    pl.run_scoped(
        phase3,
        pltpu.VMEM((VOCAB, D), BF16),
        pltpu.VMEM((TOK, D), F32),
        pltpu.VMEM((16, SPAN), F32),
        pltpu.VMEM((TOK, 256), F32),
        pltpu.VMEM((SPAN, 1024), BF16),
        pltpu.VMEM((1024, D), BF16),
        pltpu.VMEM((1024, D), BF16),
        pltpu.VMEM((TOK, 1024), BF16),
        pltpu.VMEM((TOK, D), BF16),
        pltpu.VMEM((1024, D), F32),
        pltpu.VMEM((TOK, 1024), BF16),
        pltpu.VMEM((8, SPAN), F32),
    )

    began = []

    def small_start(n, src, dst, peer):
        copy = remote(src, dst, small_send.at[n], small_recv.at[n], peer)
        copy.start()
        began.append(copy)

    def small_await(n, dst, peer):
        remote(dst, dst, small_send.at[n], small_recv.at[n], peer).wait_recv()

    small_start(0, gs, small_other, place.sibling())
    go("X9", "S5", "W4", "L6", "L7", "L8")
    small_await(0, small_other, place.sibling())
    began.pop().wait_send()
    gs[...] = (gs[...].astype(F32) + small_other[...].astype(F32)).astype(BF16)
    for i in range(1, place.inner):
        for k in range(place.outer):
            f1 = lax.rem(place.f1 + k, place.outer)
            f2 = lax.rem(place.f2 + i, place.inner)
            n = 1 + i * place.outer + k
            small_start(n, gs.at[f1 * place.inner + f2], small_inner.at[i - 1, k], place.inner_peer(i))
    go("Y9", "Z9", "W5", "S6", "S7", "S8")
    for k in list(range(1, place.outer)) + [0]:
        f1 = lax.rem(place.f1 + k, place.outer)
        tile = gs.at[f1 * place.inner + place.f2]
        total = tile[...].astype(F32)
        for i in range(1, place.inner):
            n = 1 + i * place.outer + k
            small_await(n, small_inner.at[i - 1, k], place.inner_peer(i))
            total = total + small_inner[i - 1, k].astype(F32)
        tile[...] = total.astype(BF16)
        if k:
            n = 1 + place.shards + k
            small_start(n, tile, small_outer.at[k - 1], place.outer_peer(k))
    go("L9", "W6", "W7", "W8")
    tile = gs.at[place.f]
    total = tile[...].astype(F32)
    for k in range(1, place.outer):
        n = 1 + place.shards + k
        small_await(n, small_outer.at[k - 1], place.outer_peer(k))
        total = total + small_outer[k - 1].astype(F32)
    tile[...] = total.astype(BF16)
    for p in range(1, place.planes):
        n = 1 + 2 * place.shards + p
        small_start(n, tile, small_last.at[p - 1], place.plane_peer(p))
    go("S9")
    total = tile[...].astype(F32)
    for p in range(1, place.planes):
        n = 1 + 2 * place.shards + p
        small_await(n, small_last.at[p - 1], place.plane_peer(p))
        total = total + small_last[p - 1].astype(F32)
    o_cw[...] = total[0:4, 0 : sz.d]
    for n, out in enumerate((o_cb, o_sw, o_na, o_nf)):
        out[...] = total[4 + n, 0 : sz.d]
    o_rel[...] = total[8, 0 : sz.rel]
    go("W9")
    for job in jobs:
        job.finish()
    for copy in began:
        copy.wait_send()


def body(shards, copies, *args):
    sz = Sizes(shards)
    vmem = pl.BlockSpec(memory_space=pltpu.VMEM)
    anywhere = pl.BlockSpec(memory_space=pl.ANY)
    saved = saved_shapes()
    inner = 2 if shards < 16 else 4
    outer = shards // inner
    planes = copies // 2
    n_parts = len(gather_parts(sz))
    out_grad = args[16]
    kept = pl.pallas_call(
        functools.partial(forward_kernel, sz, copies),
        out_shape=list(saved.values()),
        in_specs=[vmem] * 16,
        out_specs=[anywhere] * len(saved),
        scratch_shapes=[in_vmem(s) for s in saved.values()]
        + [
            pltpu.VMEM((shards, 16, 128), BF16),
            pltpu.VMEM((16, 128), F32),
            pltpu.VMEM((16, 1024), F32),
            pltpu.SemaphoreType.DMA((len(saved),)),
            pltpu.SemaphoreType.DMA((n_parts, 4 * shards)),
            pltpu.SemaphoreType.DMA((n_parts, 4 * shards)),
            pltpu.SemaphoreType.DMA((shards,)),
            pltpu.SemaphoreType.DMA((shards,)),
        ],
        compiler_params=pltpu.CompilerParams(collective_id=0, has_side_effects=True, vmem_limit_bytes=VMEM_LIMIT),
        name="gather_forward",
    )(*args[:16])
    kept = dict(zip(saved, kept))
    parts = reduce_parts(sz)
    sems = Reduce.sems(shards, copies)
    grads = pl.pallas_call(
        functools.partial(backward_kernel, sz, copies),
        out_shape=[shape(a.shape, F32) for a in args[2:16]],
        in_specs=[anywhere] * (1 + len(BACK_IN)),
        out_specs=[vmem] * 14,
        scratch_shapes=[
            pltpu.VMEM((VOCAB, D), BF16),
            pltpu.VMEM((4, D, D), BF16),
            pltpu.VMEM((D, 2 * FF), BF16),
            pltpu.VMEM((FF, D), BF16),
            pltpu.VMEM((shards, 16, 128), BF16),
            pltpu.VMEM((TOK, D), BF16),
            pltpu.VMEM((16, D), F32),
            pltpu.VMEM((TOK, D), F32),
            pltpu.VMEM((TOK, D), BF16),
            pltpu.VMEM((TOK, D), F32),
            pltpu.VMEM((TOK, D), F32),
            pltpu.VMEM((16, 1024), F32),
            pltpu.SemaphoreType.DMA((4, 8)),
            pltpu.SemaphoreType.DMA((len(parts), sems)),
            pltpu.SemaphoreType.DMA((len(parts), sems)),
            pltpu.VMEM((shards, 16, 128), BF16),
            pltpu.VMEM((inner - 1, outer, 16, 128), BF16),
            pltpu.VMEM((outer - 1, 16, 128), BF16),
            pltpu.VMEM((planes - 1, 16, 128), BF16),
            pltpu.SemaphoreType.DMA((2 + 2 * shards + copies,)),
            pltpu.SemaphoreType.DMA((2 + 2 * shards + copies,)),
        ]
        + [b for _, _, part in parts for b in Reduce.buffers(shards, copies, part)],
        compiler_params=pltpu.CompilerParams(collective_id=1, has_side_effects=True, vmem_limit_bytes=VMEM_LIMIT),
        name="backward_reduce",
    )(out_grad, *[kept[name] for name in BACK_IN])
    return (kept["mixed"], *grads)


def solution(mesh):
    both = P(("fsdp", "dp"), None)
    rows, line, taps = P("fsdp", None), P("fsdp"), P(None, "fsdp")
    weights = (rows, taps, line, line, line, rows, rows, rows, rows, line, line, rows, rows, rows)
    return jax.shard_map(
        functools.partial(body, mesh.shape["fsdp"], mesh.shape["dp"]),
        mesh=mesh,
        in_specs=(both, both) + weights + (both,),
        out_specs=(both,) + weights,
        check_vma=False,
    )
```

```python
import functools
import jax
import jax.numpy as jnp
from jax import lax
from jax.experimental import pallas as pl
from jax.experimental.pallas import tpu as pltpu
from jax.sharding import PartitionSpec as P

F32 = jnp.float32
BF16 = jnp.bfloat16
I32 = jnp.int32
D = 768
FF = 2048
HEADS = 12
VOCAB = 256
BUCKETS = 32
TOK = 512
BYTES = 1024
PAD = 64
SPAN = BYTES + 2 * PAD
THRESHOLDS = (12, 16, 23, 32, 46, 64, 91)
EPSILON = 1e-06
MESH = pl.DeviceIdType.MESH


class Sizes:
    def __init__(self, shards):
        self.shards = shards
        self.emb = VOCAB // shards
        self.d = D // shards
        self.ff = FF // shards
        self.rel = BUCKETS * HEADS // shards


def nn(a, b):
    return jnp.dot(a, b, preferred_element_type=F32)


def nt(a, b):
    return lax.dot_general(a, b, (((1,), (1,)), ((), ())), preferred_element_type=F32)


def tn(a, b):
    return lax.dot_general(a, b, (((0,), (0,)), ((), ())), preferred_element_type=F32)


def iota(shape, dim):
    return lax.broadcasted_iota(I32, shape, dim)


def split3_rows(row):
    hi = row.astype(BF16).astype(F32)
    mid = (row - hi).astype(BF16).astype(F32)
    low = (row - hi - mid).astype(BF16).astype(F32)
    at = iota(row.shape, 0)
    zero = jnp.zeros_like(row)
    return jnp.where(at == 0, hi, jnp.where(at == 1, mid, jnp.where(at == 2, low, zero))).astype(BF16)


def expand_smalls(sz, small):
    wide = jnp.zeros((16, D), F32)
    flat = jnp.zeros((16, BUCKETS * HEADS), F32)
    for s in range(sz.shards):
        piece = small[s]
        i, c = iota((128, D), 0), iota((128, D), 1)
        place = jnp.where((c == i + s * sz.d) & (i < sz.d), 1.0, 0.0).astype(BF16)
        wide = wide + nn(piece, place)
        i, c = iota((128, BUCKETS * HEADS), 0), iota((128, BUCKETS * HEADS), 1)
        place = jnp.where((c == i + s * sz.rel) & (i < sz.rel), 1.0, 0.0).astype(BF16)
        flat = flat + nn(piece, place)
    return wide, flat


def bucket_of(relative):
    distance = jnp.abs(relative)
    far = jnp.full(relative.shape, 8, I32)
    for threshold in THRESHOLDS:
        far = far + jnp.where(distance >= threshold, 1, 0)
    return jnp.where(distance < 8, distance, far) + jnp.where(relative > 0, 16, 0)


def offset_buckets():
    return jnp.where(
        bucket_of(iota((128, 1024), 1) - 512) == iota((128, 1024), 0), 1.0, 0.0
    ).astype(BF16)


def offset_bias(flat):
    n = BUCKETS * HEADS
    row = jnp.broadcast_to(flat[8:9, :], (16, n))
    h, c = iota((16, n), 0), iota((16, n), 1)
    mine = jnp.where(lax.rem(c, HEADS) == h, row, 0.0).astype(BF16)
    c, b = iota((n, 128), 0), iota((n, 128), 1)
    by_bucket = nn(mine, jnp.where(lax.div(c, HEADS) == b, 1.0, 0.0).astype(BF16))
    return nn(by_bucket.astype(BF16), offset_buckets())


def toeplitz(row):
    wide = jnp.broadcast_to(row, (128, 1024))
    return pltpu.roll(wide, 0, 1, stride=1, stride_axis=0)[:, 128:1024]


def key_span(block):
    return max(0, block - 2) * 128, min(4, block + 3) * 128


def band(i, seg_q, seg_p):
    r, lane = iota((128, 256), 0), iota((128, 256), 1)
    p = 128 * i + 2 * (r & 63) + (r >> 6)
    q = 128 * i - PAD + lane
    same = jnp.concatenate([seg_p, seg_p], axis=0) == seg_q
    one = jnp.where(p == q, 1.0, 0.0)
    two = jnp.where((p >> 1) == (q >> 1), 0.5, 0.0)
    third_p, third_q = (p * 43691) >> 17, (q * 43691) >> 17
    three = jnp.where(same & (third_p == third_q), 1.0, 0.0)
    four = jnp.where(same & ((p >> 2) == (q >> 2)), 1.0, 0.0)
    three = three / jnp.sum(three, axis=1, keepdims=True)
    four = four / jnp.sum(four, axis=1, keepdims=True)
    return one, two, three, four


def band_weights(averages, u):
    scores = [jnp.sum(a * u, axis=1, keepdims=True) for a in averages]
    top = jnp.maximum(jnp.maximum(scores[0], scores[1]), jnp.maximum(scores[2], scores[3]))
    raised = [jnp.exp(s - top) for s in scores]
    total = raised[0] + raised[1] + raised[2] + raised[3]
    return [e / total for e in raised]


def segments(seg_ref, seg_col):
    marked = jnp.broadcast_to(seg_ref[0:1, :].astype(F32) + 1.0, (16, TOK))
    first = jnp.where(iota((16, TOK), 0) == 0, marked, 0.0).astype(BF16)
    seg_col[...] = tn(first, jnp.ones((16, 256), BF16))
    t, j = iota((TOK, SPAN), 0), iota((TOK, SPAN), 1)
    spread = jnp.where(((j - PAD) >> 1) == t, 1.0, 0.0).astype(BF16)
    return nn(marked.astype(BF16), spread)[0:8]


def byte_tables(ids_ref, seg_pad, table):
    ids = jnp.broadcast_to(ids_ref[0:1, :].astype(F32), (8, BYTES))
    ids = pltpu.roll(jnp.concatenate([ids, jnp.zeros((8, 2 * PAD), F32)], axis=1), PAD, 1)
    kept = jnp.full((16, SPAN), -1.0, F32)
    at = iota((16, SPAN), 0)
    for k in range(4):
        turn = (2 - k) % SPAN
        near = ids if turn == 0 else pltpu.roll(ids, turn, 1)
        near_seg = seg_pad if turn == 0 else pltpu.roll(seg_pad, turn, 1)
        row = jnp.where((near_seg == seg_pad) & (seg_pad > 0.5), near, -1.0)
        kept = jnp.where(at == k, jnp.concatenate([row, row], axis=0), kept)
    kept = kept.astype(BF16)
    pick = jnp.where(iota((16, 1024), 0) == (iota((16, 1024), 1) >> 8), 1.0, 0.0).astype(BF16)
    value = (iota((128, 1024), 1) & 255).astype(F32)
    for c in range(SPAN // 128):
        spread = tn(kept[:, 128 * c : 128 * c + 128], pick)
        table[128 * c : 128 * c + 128, :] = jnp.where(spread == value, 1.0, 0.0).astype(BF16)


def tap_table(embed, wide, t_hi, t_low):
    for k in range(4):
        product = embed * wide[k : k + 1, :]
        high = product.astype(BF16)
        t_hi[256 * k : 256 * k + 256, :] = high
        t_low[256 * k : 256 * k + 256, :] = (product - high.astype(F32)).astype(BF16)


def score_row(wide, t_hi, t_low, table):
    score = jnp.broadcast_to(wide[5:6, :], (16, D)).astype(BF16)
    by_tap = nt(score, t_hi[...]) + nt(score, t_low[...])
    u = jnp.sum(nt(split3_rows(by_tap), table[...]), axis=0, keepdims=True)
    return u + jnp.sum(wide[4:5, :] * wide[5:6, :], axis=1, keepdims=True)


def rms_rows(x, gain):
    scale = lax.rsqrt(jnp.mean(x * x, axis=1, keepdims=True) + EPSILON)
    return x * scale * gain


def rms_back(x, gain, dy):
    scale = lax.rsqrt(jnp.mean(x * x, axis=1, keepdims=True) + EPSILON)
    hat = x * scale
    dg = dy * gain
    inner = jnp.mean(dg * hat, axis=1, keepdims=True)
    return scale * (dg - hat * inner), dy * hat


def gelu_parts(x):
    c = 0.7978845608028654
    square = x * x
    t = jnp.tanh(c * x * (1.0 + 0.044715 * square))
    half = 0.5 * (1.0 + t)
    slope = half + 0.5 * x * (1.0 - t * t) * (c * (1.0 + 3 * 0.044715 * square))
    return x * half, slope


def lane_half(e):
    lanes = iota((1, 128), 1)
    return (lanes < 64) if e == 0 else (lanes >= 64)


def masked(x, e):
    return jnp.where(lane_half(e), x, jnp.zeros_like(x))


def forward_mix(seg_col, rows_ref, table, mix):
    @pl.loop(0, BYTES // 128)
    def _(i):
        window = pl.ds(pl.multiple_of(128 * i, 128), 256)
        tokens = pl.ds(pl.multiple_of(64 * i, 64), 64)
        averages = band(i, rows_ref[0:1, window], seg_col[tokens, :])
        weights = band_weights(averages, rows_ref[8:9, window])
        blend = sum(wt * a for wt, a in zip(weights, averages))
        pair = 0.5 * (blend[0:64] + blend[64:128])
        mix[tokens, :] = nn(pair.astype(BF16), table[pl.ds(pl.multiple_of(128 * i, 128), 256), :]).astype(BF16)


def forward_h0(mix, t_hi, wide, h0):
    for c in range(3):
        cols = slice(256 * c, 256 * c + 256)
        h0[:, cols] = nn(mix[...], t_hi[:, cols]) + wide[4:5, cols]


def norm_into(x_ref, gain, out_ref):
    @pl.loop(0, 4)
    def _(i):
        rows = pl.ds(pl.multiple_of(128 * i, 128), 128)
        out_ref[rows, :] = rms_rows(x_ref[rows, :], gain).astype(BF16)


def forward_projection(n, w4, attn_in, qkv):
    for c in range(3):
        cols = slice(256 * c, 256 * c + 256)
        qkv[n, :, cols] = nn(attn_in[...], w4[n, :, cols]).astype(BF16)


def forward_pair(hp, qkv, bias_ref, seg_col, rows_tok, probs, ctx):
    lanes = pl.ds(pl.multiple_of(128 * hp, 128), 128)
    keys = qkv[1, :, lanes]
    values = [masked(qkv[2, :, lanes], e) for e in (0, 1)]
    bias = [toeplitz(bias_ref[pl.ds(2 * hp + e, 1), :]) for e in (0, 1)]
    for block in range(4):
        lo, hi = key_span(block)
        rows = slice(128 * block, 128 * block + 128)
        q = qkv[0, rows, lanes]
        seg_p = seg_col[rows, 0:128]
        seg_p = jnp.concatenate([seg_p] * ((hi - lo) // 128), axis=1)
        seen = seg_p == rows_tok[0:1, lo:hi]
        out = jnp.zeros((128, 128), F32)
        for e in (0, 1):
            s = nt(masked(q, e), keys[lo:hi]) * 0.125
            at = (3 - block) * 128 + lo
            s = jnp.where(seen, s + bias[e][:, at : at + hi - lo], -1e9)
            s = jnp.exp(s - jnp.max(s, axis=1, keepdims=True))
            p = (s * (1.0 / jnp.sum(s, axis=1, keepdims=True))).astype(BF16)
            probs[2 * hp + e, rows, lo:hi] = p
            if hi - lo < TOK:
                gap = slice(384, 512) if block == 0 else slice(0, 128)
                probs[2 * hp + e, rows, gap] = jnp.zeros((128, 128), BF16)
            out = out + nn(p, values[e][lo:hi])
        ctx[rows, lanes] = out.astype(BF16)


def forward_out(w4, ctx, h0, h1):
    for c in range(3):
        cols = slice(256 * c, 256 * c + 256)
        h1[:, cols] = h0[:, cols] + nn(ctx[...], w4[3, :, cols])


def ffn_chunk(c, wgu, wd, ffn_in, dl, out, dx):
    units = pl.ds(pl.multiple_of(256 * c, 256), 256)
    uppers = pl.ds(pl.multiple_of(FF + 256 * c, 256), 256)
    gate = nn(ffn_in[...], wgu[:, units])
    up = nn(ffn_in[...], wgu[:, uppers])
    dh = nt(dl[...], wd[units, :])
    act, slope = gelu_parts(gate)
    hidden = (act * up).astype(BF16)
    dgate = (dh * (slope * up)).astype(BF16)
    dup = (dh * act).astype(BF16)
    for n in range(3):
        cols = slice(256 * n, 256 * n + 256)
        out[:, cols] += nn(hidden, wd[units, cols])
        dx[:, cols] += nt(dgate, wgu[cols, units]) + nt(dup, wgu[cols, uppers])
    wd[units, :] = tn(hidden, dl[...]).astype(BF16)
    wgu[:, units] = tn(ffn_in[...], dgate).astype(BF16)
    wgu[:, uppers] = tn(ffn_in[...], dup).astype(BF16)


def backward_norm(x_ref, gain, dy_ref, add, out_ref):
    def step(i, total):
        rows = pl.ds(pl.multiple_of(128 * i, 128), 128)
        dx, dgain = rms_back(x_ref[rows, :], gain, dy_ref[rows, :])
        out_ref[rows, :] = add[rows, :].astype(F32) + dx
        return total + jnp.sum(dgain, axis=0, keepdims=True)

    return lax.fori_loop(0, 4, step, jnp.zeros((1, D), F32))


def backward_out(w4, ctx, dh1, da, dctx):
    da[...] = dh1[...].astype(BF16)
    for c in range(3):
        cols = slice(256 * c, 256 * c + 256)
        dctx[:, cols] = nt(da[...], w4[3, cols, :]).astype(BF16)
    for c in range(3):
        cols = slice(256 * c, 256 * c + 256)
        w4[3, :, cols] = tn(ctx[...], da[:, cols]).astype(BF16)


def diagonal_sums(x):
    total = x[0:8, :]
    for a in range(1, 16):
        total = total + pltpu.roll(x[8 * a : 8 * a + 8, :], 1024 - 8 * a, 1)
    row = iota((8, 1024), 0)
    for bit in (1, 2, 4):
        total = jnp.where((row & bit) != 0, pltpu.roll(total, 1024 - bit, 1), total)
    return jnp.sum(total, axis=0, keepdims=True)


def backward_pair(hp, qkv, probs, ctx, dctx, dqkv, by_offset, ds_ref, bias_sum):
    lanes = pl.ds(pl.multiple_of(128 * hp, 128), 128)
    q, keys, values = (qkv[n, :, lanes] for n in range(3))
    dc = dctx[:, lanes]
    inner = dc.astype(F32) * ctx[:, lanes].astype(F32)
    dk = jnp.zeros((TOK, 128), F32)
    dv = jnp.zeros((TOK, 128), F32)
    for e in (0, 1):
        p_ref = probs.at[e]
        bias_sum[...] = jnp.zeros_like(bias_sum)
        for block in range(4):
            lo, hi = key_span(block)
            rows = slice(128 * block, 128 * block + 128)
            delta = jnp.sum(masked(inner[rows], e), axis=1, keepdims=True)
            dp = nt(masked(dc[rows], e), values[lo:hi])
            ds = p_ref[rows, lo:hi].astype(F32) * (dp - delta)
            at = (3 - block) * 128 + lo
            bias_sum[:, at : at + hi - lo] += ds
            ds_ref[e, rows, lo:hi] = ds.astype(BF16)
            if hi - lo < TOK:
                gap = slice(384, 512) if block == 0 else slice(0, 128)
                ds_ref[e, rows, gap] = jnp.zeros((128, 128), BF16)
        dv = dv + tn(p_ref[...], masked(dc, e))
        dk = dk + tn(ds_ref[e], masked(q, e))
        by_offset[pl.ds(2 * hp + e, 1), :] = diagonal_sums(bias_sum)
    dq = jnp.concatenate(
        [
            nn(ds_ref[0, 128 * b : 128 * b + 128, :], masked(keys, 0))
            + nn(ds_ref[1, 128 * b : 128 * b + 128, :], masked(keys, 1))
            for b in range(4)
        ],
        axis=0,
    )
    dqkv[0, :, lanes] = (dq * 0.125).astype(BF16)
    dqkv[1, :, lanes] = (dk * 0.125).astype(BF16)
    dqkv[2, :, lanes] = dv.astype(BF16)


def bias_gradient(by_offset):
    buckets = bucket_of(iota((128, 1024), 1) - 384)
    pick = jnp.where(buckets == iota((128, 1024), 0), 1.0, 0.0).astype(BF16)
    total = jnp.zeros((16, 128), F32)
    rest = by_offset
    for _ in range(3):
        part = rest.astype(BF16)
        total = total + nt(part, pick)
        rest = rest - part.astype(F32)
    n = BUCKETS * HEADS
    b, c = iota((128, n), 0), iota((128, n), 1)
    place = jnp.where(lax.div(c, HEADS) == b, 1.0, 0.0).astype(BF16)
    spread = jnp.zeros((16, n), F32)
    rest = total
    for _ in range(3):
        part = rest.astype(BF16)
        spread = spread + nn(part, place)
        rest = rest - part.astype(F32)
    h, c = iota((16, n), 0), iota((16, n), 1)
    return jnp.sum(jnp.where(lax.rem(c, HEADS) == h, spread, 0.0), axis=0, keepdims=True)


def backward_projection(n, first, w4, attn_in, dqkv, dx):
    for c in range(3):
        cols = slice(256 * c, 256 * c + 256)
        part = nt(dqkv[n], w4[n, cols, :])
        dx[:, cols] = part if first else dx[:, cols] + part
    for c in range(3):
        cols = slice(256 * c, 256 * c + 256)
        w4[n, :, cols] = tn(attn_in[...], dqkv[n, :, cols]).astype(BF16)


def backward_near(t_hi, dh0, dh0_low, q_ref):
    dh0_low[...] = dh0[...].astype(BF16)
    for c in range(4):
        at = 256 * (c % 2)
        q_ref[c // 2, :, at : at + 256] = nt(dh0_low[...], t_hi[256 * c : 256 * c + 256, :]).astype(BF16)


def backward_mix(wide, seg_col, rows_ref, table, dh0, q_ref, du_ref):
    du_ref[...] = jnp.zeros_like(du_ref)

    @pl.loop(0, BYTES // 128)
    def _(i):
        window = pl.ds(pl.multiple_of(128 * i, 128), 256)
        tokens = pl.ds(pl.multiple_of(64 * i, 64), 64)
        averages = band(i, rows_ref[0:1, window], seg_col[tokens, :])
        weights = band_weights(averages, rows_ref[8:9, window])
        near = jnp.sum(dh0[tokens, :] * wide[4:5, :], axis=1, keepdims=True)
        for n in range(2):
            near = near + nt(q_ref[n, tokens, :], table[window, 512 * n : 512 * n + 512])
        near = jnp.concatenate([near, near], axis=0) * 0.5
        dws = [jnp.sum(a * near, axis=1, keepdims=True) for a in averages]
        mean = sum(wt * dw for wt, dw in zip(weights, dws))
        total = sum((wt * (dw - mean)) * a for wt, dw, a in zip(weights, dws, averages))
        du_ref[0:1, window] += jnp.sum(total, axis=0, keepdims=True)


def backward_taps(we, wide, table, t_hi, t_low, mix, dh0, dh0_low, du_ref):
    du = du_ref[0:1, :]
    du_sum = jnp.sum(du, axis=1, keepdims=True)
    by_tap = jnp.sum(nn(split3_rows(jnp.broadcast_to(du, (16, SPAN))), table[...]), axis=0, keepdims=True)
    parts = split3_rows(jnp.broadcast_to(by_tap, (16, 1024)))
    score = jnp.broadcast_to(wide[5:6, :], (16, D)).astype(BF16)
    dscore = jnp.sum(nn(parts, t_hi[...]) + nn(parts, t_low[...]), axis=0, keepdims=True) + du_sum * wide[4:5, :]
    dconv_b = jnp.sum(dh0[...], axis=0, keepdims=True) + du_sum * wide[5:6, :]
    dconv = [[] for _ in range(4)]
    for c in range(3):
        cols = slice(256 * c, 256 * c + 256)
        embed = we[:, cols].astype(F32)
        dembed = jnp.zeros((VOCAB, 256), F32)
        for k in range(4):
            rows = slice(256 * k, 256 * k + 256)
            dt = tn(mix[:, rows], dh0_low[:, cols]) + tn(parts[:, rows], score[:, cols])
            dembed = dembed + dt * wide[k : k + 1, cols]
            dconv[k].append(jnp.sum(dt * embed, axis=0, keepdims=True))
        we[:, cols] = dembed.astype(BF16)
    return [jnp.concatenate(d, axis=1) for d in dconv], dconv_b, dscore


def pack_smalls(sz, rows, flat, out):
    at = iota((16, D), 0)
    wide = jnp.zeros((16, D), F32)
    for n, row in enumerate(rows):
        wide = jnp.where(at == n, jnp.broadcast_to(row, (16, D)), wide)
    wide = wide.astype(BF16)
    n = BUCKETS * HEADS
    rel = jnp.where(iota((16, n), 0) == 8, jnp.broadcast_to(flat, (16, n)), 0.0).astype(BF16)
    for s in range(sz.shards):
        c, i = iota((D, 128), 0), iota((D, 128), 1)
        place = jnp.where((c == i + s * sz.d) & (i < sz.d), 1.0, 0.0).astype(BF16)
        c, i = iota((n, 128), 0), iota((n, 128), 1)
        place_rel = jnp.where((c == i + s * sz.rel) & (i < sz.rel), 1.0, 0.0).astype(BF16)
        out[s] = (nn(wide, place) + nn(rel, place_rel)).astype(BF16)


REDUCE_ORDER = ("g0", "g1", "d0", "g2", "g3", "d1", "o", "v", "k", "q", "e")
LONE = {"e": 0, "q": 128, "k": 128, "v": 128, "o": 128, "d0": 128, "g0": 256, "g1": 128, "d1": 128, "g2": 128, "g3": 0}
REDUCE_LONE = {"e": 0, "q": 128, "k": 128, "v": 128, "o": 128, "d0": 128, "g0": 128, "g1": 128, "d1": 128, "g2": 128, "g3": 256}
PLAN = {
    "start": ("Zm", "Ze",),
    "cast0": ("Zq",),
    "cast1": ("Zk",),
    "cast2": ("Zv",),
    "cast4": ("Ym",),
    "t1": ("Ye",),
    "t2": ("Zo", "Yq", "Xe", "Ce", "Zd0",),
    "t3": ("Yk",),
    "t4": ("Xq", "Yv", "Zg0",),
    "t5": ("Xk", "Zg1", "Yo", "Cq", "Xv",),
    "p0": ("Zd1", "Yd0", "Ck", "Xo",),
    "p1": ("Yg0", "Cv", "Zg2",),
    "p2": ("Xd0", "Co",),
    "a0": ("Yg1", "Zg3", "Xg0",),
    "a2": ("Cd0", "Yd1",),
    "a3": ("Xg1",),
    "a4": ("Yg2",),
    "a5": ("Cg0", "Xd1",),
    "f0": ("Cg1",),
    "f1": ("Xg2", "Yg3", "cg0",),
    "f2": ("Cd1", "xg0",),
    "f3": ("cg1", "cd0", "Cg2", "xg1", "xd0",),
    "f4": ("Xg3", "Cg3", "yg0",),
    "f5": ("yg1", "cg2",),
    "f6": ("xg2",),
    "f7": ("yd0", "cg3", "zg0", "cd1",),
    "g0": ("xg3",),
    "g1": ("yg2", "xd1", "co",),
    "b0": ("zg1", "xo",),
    "b1": ("lg0",),
    "b3": ("zd0", "yg3",),
    "b4": ("lg1",),
    "q2": ("zg2", "yd1", "cv",),
    "q1": ("ld0", "xv", "ck",),
    "q0": ("zg3", "yo", "sg0", "xk", "cq",),
    "g2": ("wg0", "sg1",),
    "g3": ("wg1", "sd0", "lg2", "zd1", "wd0", "xq",),
    "g4": ("lg3", "zo", "yv",),
    "g5": ("ce",),
    "g6": ("yk", "xe", "ye", "sg2", "ld1", "cm", "wg2", "xm", "zv",),
    "end": ("lo", "yq", "sg3", "zk", "wg3", "sd1", "so", "wd1", "ze", "lv", "wo", "zm", "sv", "lk", "zq", "wv", "le", "lm", "sk", "wk", "se", "sm", "we", "lq", "sq", "wq",),
}


class Place:
    def __init__(self, shards, copies):
        self.shards, self.copies = shards, copies
        self.inner = 2 if shards < 16 else 4
        self.outer = shards // self.inner
        self.planes = copies // 2
        f, d = lax.axis_index("fsdp"), lax.axis_index("dp")
        self.f, self.d = f, d
        self.f1, self.f2 = lax.div(f, self.inner), lax.rem(f, self.inner)
        self.x, self.core = lax.div(d, 2), lax.rem(d, 2)

    def shard(self, k, i):
        f1 = lax.rem(self.f1 + (self.outer - k), self.outer)
        f2 = lax.rem(self.f2 + (self.inner - i), self.inner)
        return f1 * self.inner + f2

    def outer_peer(self, k):
        return (lax.rem(self.f1 + k, self.outer) * self.inner + self.f2, self.d)

    def inner_peer(self, i):
        return (self.f1 * self.inner + lax.rem(self.f2 + i, self.inner), self.d)

    def plane_peer(self, p):
        return (self.f, lax.rem(self.x + p, self.planes) * 2 + self.core)

    def sibling(self):
        return (self.f, self.x * 2 + (1 - self.core))

    def barrier(self):
        peers = [self.outer_peer(k) for k in range(1, self.outer)]
        peers += [self.inner_peer(i) for i in range(1, self.inner)]
        peers += [self.plane_peer(p) for p in range(1, self.planes)]
        peers += [self.sibling()]
        sem = pltpu.get_barrier_semaphore()
        for peer in peers:
            pl.semaphore_signal(sem, inc=1, device_id=peer, device_id_type=MESH)
        pl.semaphore_wait(sem, len(peers))


def aligned(value, unit):
    return value if isinstance(value, int) else pl.multiple_of(value, unit)


def remote(src, dst, send, recv, peer):
    return pltpu.make_async_remote_copy(
        src_ref=src, dst_ref=dst, send_sem=send, recv_sem=recv, device_id=peer, device_id_type=MESH
    )


class Part:
    def __init__(self, first, rows, base, gap, half, lone):
        self.first, self.rows = first, rows
        self.base, self.gap, self.half, self.lone = base, gap, half, lone

    def split(self, place):
        return self.lone if place.planes == 2 else 0

    def wide(self, place):
        return self.half - self.split(place)

    def view(self, ref, shard, column, width):
        row = aligned(shard * self.rows + self.first, 16)
        return ref.at[pl.ds(row, self.rows), pl.ds(aligned(column, 128), width)]

    def every(self, ref, place, column, width):
        return ref.at[pl.ds(self.first, place.shards * self.rows), pl.ds(aligned(column, 128), width)]

    def column(self, ref, place, f2, start, width):
        block = ref.at[pl.ds(self.first, place.shards * self.rows), :]
        block = block.reshape(place.outer, place.inner * self.rows, block.shape[1])
        row = aligned(f2 * self.rows, 16)
        return block.at[:, pl.ds(row, self.rows), pl.ds(aligned(start, 128), width)]

    def start(self, place):
        return place.core * self.gap + self.base

    def start_other(self, place):
        return (1 - place.core) * self.gap + self.base

    def mine(self, ref, place, shard):
        return self.view(ref, shard, self.start(place) + place.x * self.split(place), self.wide(place))

    def moved(self, ref, place, f2):
        return self.column(ref, place, f2, self.start(place) + place.x * self.split(place), self.wide(place))

    def kept(self, ref, place):
        return self.every(ref, place, self.start(place) + place.x * self.wide(place), self.lone)

    def lacked(self, ref, place):
        return self.every(ref, place, self.start(place) + (1 - place.x) * self.wide(place), self.lone)


class Sends:
    def _start(self, n, src, dst, peer):
        def make():
            return remote(src(), dst(), self.send.at[n], self.recv.at[n], peer())

        make().start()
        self.sent.append(make)

    def _await(self, n, dst, peer):
        remote(dst, dst, self.send.at[n], self.recv.at[n], peer).wait_recv()

    def finish(self):
        for make in self.sent:
            make().wait_send()


class Gather(Sends):
    @staticmethod
    def sems(shards):
        inner = 2 if shards < 16 else 4
        return shards // inner + inner

    def __init__(self, place, part, ref, send, recv):
        self.place, self.part, self.ref = place, part, ref
        self.send, self.recv = send, recv
        self.sent = []

    def first(self):
        place = self.place

        def own():
            return self.part.mine(self.ref, place, place.f)

        for k in range(1, place.outer):
            self._start(k - 1, own, own, functools.partial(place.outer_peer, k))

    def second(self):
        place = self.place
        for k in range(1, place.outer):
            self._await(k - 1, self.part.mine(self.ref, place, place.shard(k, 0)), place.outer_peer(k))

        def column():
            return self.part.moved(self.ref, place, place.f2)

        for i in range(1, place.inner):
            self._start(place.outer + i - 2, column, column, functools.partial(place.inner_peer, i))

    def third(self):
        place, part = self.place, self.part
        for i in range(1, place.inner):
            f2 = lax.rem(place.f2 + (place.inner - i), place.inner)
            self._await(place.outer + i - 2, part.moved(self.ref, place, f2), place.inner_peer(i))
        if part.split(place):

            def kept():
                return part.kept(self.ref, place)

            self._start(place.outer + place.inner - 2, kept, kept, functools.partial(place.plane_peer, 1))

    def fourth(self):
        place, part = self.place, self.part
        if part.split(place):
            self._await(place.outer + place.inner - 2, part.lacked(self.ref, place), place.plane_peer(1))

        def half():
            return part.every(self.ref, place, part.start(place), part.half)

        self._start(place.outer + place.inner - 1, half, half, place.sibling)

    def fifth(self):
        place, part = self.place, self.part
        view = part.every(self.ref, place, part.start_other(place), part.half)
        self._await(place.outer + place.inner - 1, view, place.sibling())


def add_rows(target, source, rows, step):
    if rows <= step:
        target[...] = (target[...].astype(F32) + source[...].astype(F32)).astype(BF16)
        return

    @pl.loop(0, rows // step)
    def _(n):
        at = pl.ds(pl.multiple_of(n * step, step), step)
        target[at, :] = (target[at, :].astype(F32) + source[at, :].astype(F32)).astype(BF16)


class Reduce(Sends):
    @staticmethod
    def buffers(shards, copies, part):
        inner = 2 if shards < 16 else 4
        outer = shards // inner
        planes = copies // 2
        split = part.lone if planes == 2 else 0
        wide = part.half - split
        shapes = [
            (shards * part.rows, part.half),
            (shards * part.rows, split) if split else (16, 128),
            (inner - 1, outer, part.rows, wide),
            (outer - 1, part.rows, wide),
            (planes - 1, part.rows, wide),
        ]
        return [pltpu.VMEM(s, BF16) for s in shapes]

    @staticmethod
    def sems(shards, copies):
        inner = 2 if shards < 16 else 4
        return shards // inner + inner + copies // 2 + 2

    def __init__(self, place, part, ref, out, bufs, send, recv):
        self.place, self.part, self.ref, self.out = place, part, ref, out
        self.from_core, self.from_plane, self.from_inner, self.from_outer, self.last = bufs
        self.send, self.recv = send, recv
        self.sent = []
        self.rows = place.shards * part.rows

    def _columns(self, column, width):
        return self.part.every(self.ref, self.place, column, width)

    def first(self):
        place, part = self.place, self.part
        self._start(
            0,
            lambda: self._columns(part.start_other(place), part.half),
            lambda: self.from_core,
            place.sibling,
        )

    def second(self):
        place, part = self.place, self.part
        self._await(0, self.from_core, place.sibling())
        target = self._columns(part.start(place), part.half)
        add_rows(target, self.from_core, self.rows, 64)
        if part.split(place):
            self._start(
                1,
                lambda: self._columns(part.start(place) + (1 - place.x) * part.wide(place), part.lone),
                lambda: self.from_plane,
                functools.partial(place.plane_peer, 1),
            )
        else:
            self._inner()

    def _inner(self):
        place, part = self.place, self.part
        for i in range(1, place.inner):
            self._start(
                1 + i,
                lambda i=i: part.moved(self.ref, place, lax.rem(place.f2 + i, place.inner)),
                lambda i=i: self.from_inner.at[i - 1],
                functools.partial(place.inner_peer, i),
            )

    def third(self):
        place, part = self.place, self.part
        if part.split(place):
            self._await(1, self.from_plane, place.plane_peer(1))
            target = self._columns(part.start(place) + place.x * part.wide(place), part.lone)
            add_rows(target, self.from_plane, self.rows, 128)
            self._inner()

    def fourth(self):
        place, part = self.place, self.part
        for i in range(1, place.inner):
            self._await(1 + i, self.from_inner.at[i - 1], place.inner_peer(i))
        for k in list(range(1, place.outer)) + [0]:

            def mine(k=k):
                f1 = lax.rem(place.f1 + k, place.outer)
                return part.mine(self.ref, place, f1 * place.inner + place.f2)

            target = mine()
            total = target[...].astype(F32)
            for i in range(1, place.inner):
                total = total + self.from_inner[i - 1, lax.rem(place.f1 + k, place.outer)].astype(F32)
            target[...] = total.astype(BF16)
            if k:
                self._start(
                    place.inner + k,
                    mine,
                    functools.partial(lambda k: self.from_outer.at[k - 1], k),
                    functools.partial(place.outer_peer, k),
                )

    def fifth(self):
        place, part = self.place, self.part
        for k in range(1, place.outer):
            self._await(place.inner + k, self.from_outer.at[k - 1], place.outer_peer(k))
        target = part.mine(self.ref, place, place.f)
        total = target[...].astype(F32)
        for k in range(1, place.outer):
            total = total + self.from_outer[k - 1].astype(F32)
        target[...] = total.astype(BF16)
        for p in range(1, place.planes):
            self._start(
                place.inner + place.outer - 1 + p,
                lambda: part.mine(self.ref, place, place.f),
                functools.partial(lambda p: self.last.at[p - 1], p),
                functools.partial(place.plane_peer, p),
            )

    def sixth(self):
        place, part = self.place, self.part
        for p in range(1, place.planes):
            self._await(place.inner + place.outer - 1 + p, self.last.at[p - 1], place.plane_peer(p))
        mine = part.mine(self.ref, place, place.f)[...].astype(F32)
        start = part.start(place)

        def put(column, width, values):
            self.out[:, pl.ds(aligned(start + column, 128), width)] = values.astype(BF16)

        if part.split(place):
            theirs = self.last[0].astype(F32)
            lone, wide, both = part.lone, part.wide(place), part.half - 2 * part.lone
            low = place.x == 0
            if both:
                shared = jnp.where(low, mine[:, lone:], mine[:, :both]) + jnp.where(low, theirs[:, :both], theirs[:, lone:])
                put(lone, both, shared)
            put(0, lone, jnp.where(low, mine[:, 0:lone], theirs[:, 0:lone]))
            put(wide, lone, jnp.where(low, theirs[:, both:], mine[:, both:]))
        else:
            for p in range(1, place.planes):
                mine = mine + self.last[p - 1].astype(F32)
            put(0, part.half, mine)
        n = place.inner + place.outer + place.planes - 1

        def whole():
            return self.out.at[:, pl.ds(aligned(part.start(place), 128), part.half)]

        self._start(n, whole, whole, place.sibling)

    def seventh(self):
        place, part = self.place, self.part
        view = self.out.at[:, pl.ds(aligned(part.start_other(place), 128), part.half)]
        self._await(place.inner + place.outer + place.planes - 1, view, place.sibling())


class SmallGather(Sends):
    def __init__(self, place, small, send, recv):
        self.place, self.small, self.send, self.recv = place, small, send, recv
        self.sent = []

    def _column(self, f2):
        place = self.place
        return self.small.reshape(place.outer, place.inner * 16, 128).at[:, pl.ds(aligned(f2 * 16, 16), 16), :]

    def first(self):
        place = self.place

        def own():
            return self.small.at[place.f]

        for k in range(1, place.outer):
            self._start(k - 1, own, own, functools.partial(place.outer_peer, k))

    def second(self):
        place = self.place
        for k in range(1, place.outer):
            self._await(k - 1, self.small.at[place.shard(k, 0)], place.outer_peer(k))

        def column():
            return self._column(place.f2)

        for i in range(1, place.inner):
            self._start(place.outer + i - 2, column, column, functools.partial(place.inner_peer, i))

    def fifth(self):
        place = self.place
        for i in range(1, place.inner):
            f2 = lax.rem(place.f2 + (place.inner - i), place.inner)
            self._await(place.outer + i - 2, self._column(f2), place.inner_peer(i))


class SmallReduce(Sends):
    @staticmethod
    def buffers(shards, copies):
        inner = 2 if shards < 16 else 4
        outer, planes = shards // inner, copies // 2
        shapes = [(shards, 16, 128), (inner - 1, outer, 16, 128), (outer - 1, 16, 128), (planes - 1, 16, 128)]
        return [pltpu.VMEM(s, BF16) for s in shapes]

    def __init__(self, place, gs, out, bufs, send, recv):
        self.place, self.gs, self.out, self.send, self.recv = place, gs, out, send, recv
        self.from_core, self.from_inner, self.from_outer, self.last = bufs
        self.sent = []

    def first(self):
        self._start(0, lambda: self.gs, lambda: self.from_core, self.place.sibling)

    def second(self):
        place = self.place
        self._await(0, self.from_core, place.sibling())
        self.sent.pop()().wait_send()
        self.gs[...] = (self.gs[...].astype(F32) + self.from_core[...].astype(F32)).astype(BF16)

        def column(i):
            f2 = lax.rem(place.f2 + i, place.inner)
            return self.gs.reshape(place.outer, place.inner * 16, 128).at[:, pl.ds(aligned(f2 * 16, 16), 16), :]

        for i in range(1, place.inner):
            self._start(
                i,
                functools.partial(column, i),
                lambda i=i: self.from_inner.at[i - 1],
                functools.partial(place.inner_peer, i),
            )

    def _tile(self, k):
        place = self.place
        return self.gs.at[lax.rem(place.f1 + k, place.outer) * place.inner + place.f2]

    def fourth(self):
        place = self.place
        for i in range(1, place.inner):
            self._await(i, self.from_inner.at[i - 1], place.inner_peer(i))
        for k in list(range(1, place.outer)) + [0]:
            total = self._tile(k)[...].astype(F32)
            for i in range(1, place.inner):
                total = total + self.from_inner[i - 1, lax.rem(place.f1 + k, place.outer)].astype(F32)
            self._tile(k)[...] = total.astype(BF16)
            if k:
                self._start(
                    place.inner - 1 + k,
                    functools.partial(self._tile, k),
                    lambda k=k: self.from_outer.at[k - 1],
                    functools.partial(place.outer_peer, k),
                )

    def fifth(self):
        place = self.place
        total = self._tile(0)[...].astype(F32)
        for k in range(1, place.outer):
            self._await(place.inner - 1 + k, self.from_outer.at[k - 1], place.outer_peer(k))
            total = total + self.from_outer[k - 1].astype(F32)
        self._tile(0)[...] = total.astype(BF16)
        for p in range(1, place.planes):
            self._start(
                place.inner + place.outer - 2 + p,
                functools.partial(self._tile, 0),
                lambda p=p: self.last.at[p - 1],
                functools.partial(place.plane_peer, p),
            )

    def sixth(self):
        place = self.place
        total = self._tile(0)[...].astype(F32)
        for p in range(1, place.planes):
            self._await(place.inner + place.outer - 2 + p, self.last.at[p - 1], place.plane_peer(p))
            total = total + self.last[p - 1].astype(F32)
        self.out[...] = total


VMEM_LIMIT = 64 * 1024 * 1024 - 65536


def gather_parts(sz, lone=LONE):
    parts = {"e": ("we", None, Part(0, sz.emb, 0, 384, 384, lone["e"]))}
    for n, name in enumerate("qkvo"):
        parts[name] = ("w4", n, Part(0, sz.d, 0, 384, 384, lone[name]))
    blocks = sz.ff // 128
    for j in range(4):
        if j % (4 // blocks) == 0:
            first = 128 * sz.shards * (j * blocks // 4)
            name = "d%d" % (j * blocks // 4)
            parts[name] = ("wd", None, Part(first, 128, 0, 384, 384, lone[name]))
        name = "g%d" % j
        parts[name] = ("wgu", None, Part(0, sz.d, 512 * j, FF, 512, lone[name]))
    return parts


def reduce_parts(sz):
    parts = gather_parts(sz, REDUCE_LONE)
    return {name: parts[name] for name in REDUCE_ORDER if name in parts}


class Schedule:
    def __init__(self, gathers, reduces, plan):
        self.jobs = {"G": gathers, "R": reduces}
        self.plan = plan
        self.done = []

    def go(self, step):
        kind, name = step[0], step[1:]
        gather = kind.isupper()
        job = self.jobs["G" if gather else "R"][name]
        step_of = {
            "Z": "first", "Y": "second", "X": "third", "C": "fourth", "W": "fifth", "F": "finish",
            "c": "first", "x": "second", "y": "third", "z": "fourth", "l": "fifth", "s": "sixth", "w": "seventh",
        }
        if step in self.done:
            return
        order = "ZYXCWF" if gather else "cxyzlsw"
        before = order[: order.index(kind)]
        missing = [b for b in before if hasattr(job, step_of[b]) and b + name not in self.done]
        for b in missing:
            self.go(b + name)
        if hasattr(job, step_of[kind]):
            getattr(job, step_of[kind])()
        self.done.append(step)

    def hook(self, name):
        for step in self.plan.get(name, ()):
            if step[1:] in self.jobs["G" if step[0].isupper() else "R"]:
                self.go(step)

    def need(self, *steps):
        for step in steps:
            self.go(step)

    def rest(self):
        for kind in "cxyzlsw":
            for name in self.jobs["R"]:
                self.go(kind + name)
        for job in list(self.jobs["R"].values()):
            job.finish()


def step_kernel(sz, copies, *refs):
    (ids, seg, embed, conv_w, conv_b, score_w, norm_attn, w_q, w_k, w_v, w_o, rel, norm_ffn, w_g, w_u, w_d, dl_h) = refs[:17]
    mixed_o, re_o, r4_o, rgu_o, rd_o, tile_o = refs[17:23]
    refs = refs[23:]
    (we, w4, wgu, wd, re, r4, rgu, rd, tile, small, gs, stage_small) = refs[:12]
    refs = refs[12:]
    (attn_in, qkv, probs, ctx, h0, h1, ffn_in, table, t_hi, t_low, mix, rows_ref, seg_col, wide_ref) = refs[:14]
    (bias_ref, mixed, dl, dx, dh1, dctx, da, ds_ref, bias_sum, by_off, du_ref) = refs[14:25]
    in_sems, out_sems, send, recv, r_send, r_recv, small_send, small_recv, sr_send, sr_recv = refs[25:35]
    buffers = refs[35:]
    place = Place(sz.shards, copies)
    f = place.f
    arrays = dict(we=we, w4=w4, wgu=wgu, wd=wd)

    gathers = {"m": SmallGather(place, small, small_send, small_recv)}
    for n, (job, (name, lead, part)) in enumerate(gather_parts(sz).items()):
        ref = arrays[name] if lead is None else arrays[name].at[lead]
        gathers[job] = Gather(place, part, ref, send.at[n], recv.at[n])
    reduces = {}
    for n, (job, (name, lead, part)) in enumerate(reduce_parts(sz).items()):
        ref = arrays[name] if lead is None else arrays[name].at[lead]
        if name == "wd":
            block = part.first // (128 * sz.shards)
            out = rd.at[128 * block : 128 * block + 128, :]
        else:
            out = dict(we=re, w4=r4, wgu=rgu)[name]
            out = out if lead is None else out.at[lead]
        reduces[job] = Reduce(place, part, ref, out, buffers[5 * n : 5 * n + 5], r_send.at[n], r_recv.at[n])
    reduces["m"] = SmallReduce(place, gs, tile, buffers[5 * len(reduces) :], sr_send, sr_recv)
    sched = Schedule(gathers, reduces, PLAN)
    hook, need = sched.hook, sched.need

    mine = pl.ds(pl.multiple_of(place.core * 384, 128), 384)
    loads = []
    row = 0
    for n, (w, count) in enumerate(
        ((embed, sz.emb), (w_q, sz.d), (w_k, sz.d), (w_v, sz.d), (w_o, sz.d), (w_d, sz.ff))
    ):
        if n == 5:
            staged = dx.at[0:count, 384:768]
        else:
            staged = dx.at[row : row + count, 0:384]
        copy = pltpu.make_async_copy(w.at[:, mine], staged, in_sems.at[n])
        copy.start()
        loads.append((copy, staged))
        row += count

    def gu_copies(w):
        found = []
        for n in range(3):
            width = min(D, FF - n * D)
            staged = dh1.at[n * sz.d : n * sz.d + sz.d, 0:width]
            found.append(pltpu.make_async_copy(w.at[:, n * D : n * D + width], staged, in_sems.at[8 + n]))
        return found

    for core, w in enumerate((w_g, w_u)):

        @pl.when(place.core == core)
        def _(w=w):
            for copy in gu_copies(w):
                copy.start()

    dl_copy = pltpu.make_async_copy(dl_h, dl, in_sems.at[7])
    dl_copy.start()

    def own(rows, first=0):
        return pl.ds(pl.multiple_of(first + f * rows, 16), rows)

    def cast(n, name, target):
        copy, staged = loads[n]
        copy.wait()
        target[...] = staged[:, moved(name, 0)].astype(BF16)

    stage_small[...] = jnp.zeros_like(stage_small)
    stage_small[0:4, 0 : sz.d] = conv_w[...]
    for n, vector in enumerate((conv_b, score_w, norm_attn, norm_ffn)):
        stage_small[4 + n : 5 + n, 0 : sz.d] = vector[...].reshape(1, sz.d)
    stage_small[8:9, 0 : sz.rel] = rel[...].reshape(1, sz.rel)
    small[f] = stage_small[...].astype(BF16)

    def moved(name, start):
        split = LONE[name] if place.planes == 2 else 0
        return pl.ds(aligned(start + place.x * split, 128), 384 - split)

    cast(0, "e", we.at[own(sz.emb), moved("e", place.core * 384)])
    place.barrier()
    hook("start")
    for n in range(4):
        cast(n + 1, "qkvo"[n], w4.at[n, own(sz.d), moved("qkvo"[n], place.core * 384)])
        hook("cast%d" % n)
    copy, staged = loads[5]
    copy.wait()
    for j in range(sz.ff // 128):
        rows = own(128, j * 128 * sz.shards)
        name = "d%d" % j
        wd[rows, moved(name, place.core * 384)] = staged[128 * j : 128 * j + 128, moved(name, 0)].astype(BF16)
    hook("cast4")
    for copy in gu_copies(w_g):
        copy.wait()
    blocks = sz.ff // 128
    for j in range(blocks):
        for s in range(sz.shards):
            n, at = divmod(s * sz.ff + 128 * j, D)
            column = 128 * (j * sz.shards + s)
            lone = LONE["g%d" % (column // 512)] if place.planes == 2 else 0

            def put(n=n, at=at, column=place.core * FF + column):
                values = dh1[n * sz.d : n * sz.d + sz.d, at : at + 128].astype(BF16)
                wgu[own(sz.d), pl.ds(pl.multiple_of(column, 128), 128)] = values

            if column % 512 < lone:
                pl.when(place.x == 0)(put)
            elif column % 512 >= 512 - lone:
                pl.when(place.x == 1)(put)
            else:
                put()
    hook("cast5")

    seg_pad = segments(seg, seg_col)
    hook("t0")
    byte_tables(ids, seg_pad, table)
    hook("t1")
    need("Wm")
    wide, flat = expand_smalls(sz, small)
    wide_ref[...] = wide
    bias_ref[...] = offset_bias(flat)
    hook("t2")
    need("We")
    tap_table(we[...].astype(F32), wide, t_hi, t_low)
    rows_ref[0:8, :] = seg_pad
    rows_ref[8:16, :] = jnp.broadcast_to(score_row(wide, t_hi, t_low, table), (8, SPAN))
    hook("t3")
    forward_mix(seg_col, rows_ref, table, mix)
    hook("t4")
    forward_h0(mix, t_hi, wide, h0)
    norm_into(h0, wide_ref[6:7, :], attn_in)
    hook("t5")
    for n in range(3):
        need("W" + "qkv"[n])
        forward_projection(n, w4, attn_in, qkv)
        hook("p%d" % n)
    rows_tok = seg[0:1, :].astype(F32) + 1.0

    @pl.loop(0, 6)
    def _(hp):
        forward_pair(hp, qkv, bias_ref, seg_col, rows_tok, probs, ctx)
        for n in range(6):
            if PLAN.get("a%d" % n):
                pl.when(hp == n)(functools.partial(hook, "a%d" % n))

    need("Wo")
    forward_out(w4, ctx, h0, h1)
    norm_into(h1, wide_ref[7:8, :], ffn_in)
    dh1[...] = h1[...]
    dx[...] = jnp.zeros_like(dx)
    dl_copy.wait()
    hook("o")

    for j in range(4):
        need("Wd%d" % (j * blocks // 4), "Wg%d" % j)
        if j % (4 // blocks) == 0:
            need("Fd%d" % (j * blocks // 4))
        need("Fg%d" % j)
        for c in (2 * j, 2 * j + 1):
            ffn_chunk(c, wgu, wd, ffn_in, dl, dh1, dx)
            hook("f%d" % c)
    mixed[...] = dh1[...].astype(BF16)
    mixed_copy = pltpu.make_async_copy(mixed, mixed_o, out_sems.at[0])
    mixed_copy.start()

    dnorm_ffn = backward_norm(h1, wide_ref[7:8, :], dx, dl, dh1)
    hook("g0")
    need("Fo")
    backward_out(w4, ctx, dh1, da, dctx)
    hook("g1")
    by_off[...] = jnp.zeros_like(by_off)
    bias_sum[...] = jnp.zeros_like(bias_sum)

    @pl.loop(0, 6)
    def _(hp):
        backward_pair(hp, qkv, probs.at[pl.ds(2 * hp, 2)], ctx, dctx, qkv, by_off, ds_ref, bias_sum)
        for n in range(6):
            if PLAN.get("b%d" % n):
                pl.when(hp == n)(functools.partial(hook, "b%d" % n))

    for n in (2, 1, 0):
        need("F" + "qkv"[n])
        backward_projection(n, n == 2, w4, attn_in, qkv, dx)
        hook("q%d" % n)
    dnorm_attn = backward_norm(h0, wide_ref[6:7, :], dx, dh1, dx)
    hook("g2")
    backward_near(t_hi, dx, da, probs)
    hook("g3")
    wide = wide_ref[...]
    backward_mix(wide, seg_col, rows_ref, table, dx, probs, du_ref)
    hook("g4")
    need("Fe", "Fm")
    dconv, dconv_b, dscore = backward_taps(we, wide, table, t_hi, t_low, mix, dx, da, du_ref)
    hook("g5")
    pack_smalls(sz, dconv + [dconv_b, dscore, dnorm_attn, dnorm_ffn], bias_gradient(by_off[...]), gs)
    hook("g6")
    hook("end")
    sched.rest()
    outs = [(re, re_o), (r4, r4_o), (rgu, rgu_o), (rd, rd_o), (tile, tile_o)]
    last = [pltpu.make_async_copy(a, b, out_sems.at[n + 1]) for n, (a, b) in enumerate(outs)]
    for copy in last:
        copy.start()
    for copy in [mixed_copy] + last:
        copy.wait()


def unpack_kernel(sz, mixed, re, r4, rgu, rd, tile, *outs):
    o_mixed, o_e, o_cw, o_cb, o_sw, o_na, o_q, o_k, o_v, o_o, o_rel, o_nf, o_g, o_u, o_d = outs
    o_mixed[...] = mixed[...]
    o_e[...] = re[...].astype(F32)
    for n, out in enumerate((o_q, o_k, o_v, o_o)):
        out[...] = r4[n].astype(F32)
    o_d[...] = rd[...].astype(F32)
    for n, out in enumerate((o_g, o_u)):
        for j in range(sz.ff // 128):
            for s in range(sz.shards):
                at = n * FF + 128 * (j * sz.shards + s)
                out[:, s * sz.ff + 128 * j : s * sz.ff + 128 * j + 128] = rgu[:, at : at + 128].astype(F32)
    o_cw[...] = tile[0:4, 0 : sz.d]
    for n, out in enumerate((o_cb, o_sw, o_na, o_nf)):
        out[...] = tile[4 + n, 0 : sz.d]
    o_rel[...] = tile[8, 0 : sz.rel]


def shape(dims, dtype):
    return jax.ShapeDtypeStruct(dims, dtype)


def body(shards, copies, *args):
    sz = Sizes(shards)
    vmem = pl.BlockSpec(memory_space=pltpu.VMEM)
    anywhere = pl.BlockSpec(memory_space=pl.ANY)
    n_gather = len(gather_parts(sz))
    parts = [part for _, _, part in reduce_parts(sz).values()]
    sems = Reduce.sems(shards, copies)
    small_sems = Reduce.sems(shards, copies)

    def low(*dims):
        return pltpu.VMEM(dims, BF16)

    def wide(*dims):
        return pltpu.VMEM(dims, F32)

    dma = pltpu.SemaphoreType.DMA
    results = [
        shape((TOK, D), BF16),
        shape((sz.emb, D), BF16),
        shape((4, sz.d, D), BF16),
        shape((sz.d, 2 * FF), BF16),
        shape((sz.ff, D), BF16),
        shape((16, 128), F32),
    ]
    found = pl.pallas_call(
        functools.partial(step_kernel, sz, copies),
        out_shape=results,
        in_specs=[
            vmem, vmem, anywhere, vmem, vmem, vmem, vmem, anywhere, anywhere, anywhere, anywhere, vmem, vmem,
            anywhere, anywhere, anywhere, anywhere,
        ],
        out_specs=[anywhere] * len(results),
        scratch_shapes=[
            low(VOCAB, D), low(4, D, D), low(D, 2 * FF), low(FF, D),
            low(sz.emb, D), low(4, sz.d, D), low(sz.d, 2 * FF), low(sz.ff, D), wide(16, 128),
            low(shards, 16, 128), low(shards, 16, 128),
            wide(16, 128),
            low(TOK, D), low(3, TOK, D), low(HEADS, TOK, TOK), low(TOK, D), wide(TOK, D), wide(TOK, D), low(TOK, D),
            low(SPAN, 1024), low(1024, D), low(1024, D), low(TOK, 1024), wide(16, SPAN), wide(TOK, 256), wide(16, D),
            wide(16, 1024), low(TOK, D), low(TOK, D), wide(TOK, D), wide(TOK, D), low(TOK, D), low(TOK, D),
            low(2, TOK, TOK), wide(128, 1024), wide(16, 1024), wide(8, SPAN),
            dma((11,)), dma((6,)),
            dma((n_gather, Gather.sems(shards))), dma((n_gather, Gather.sems(shards))),
            dma((len(parts), sems)), dma((len(parts), sems)),
            dma((small_sems,)), dma((small_sems,)), dma((small_sems,)), dma((small_sems,)),
        ]
        + [b for part in parts for b in Reduce.buffers(shards, copies, part)]
        + SmallReduce.buffers(shards, copies),
        compiler_params=pltpu.CompilerParams(collective_id=0, has_side_effects=True, vmem_limit_bytes=VMEM_LIMIT),
        name="layer_step",
    )(*args)
    return pl.pallas_call(
        functools.partial(unpack_kernel, sz),
        out_shape=[shape((TOK, D), BF16)] + [shape(a.shape, F32) for a in args[2:16]],
        in_specs=[vmem] * 6,
        out_specs=[vmem] * 15,
        compiler_params=pltpu.CompilerParams(vmem_limit_bytes=VMEM_LIMIT),
        name="unpack",
    )(*found)


def solution(mesh):
    both = P(("fsdp", "dp"), None)
    rows, line, taps = P("fsdp", None), P("fsdp"), P(None, "fsdp")
    weights = (rows, taps, line, line, line, rows, rows, rows, rows, line, line, rows, rows, rows)
    return jax.shard_map(
        functools.partial(body, mesh.shape["fsdp"], mesh.shape["dp"]),
        mesh=mesh,
        in_specs=(both, both) + weights + (both,),
        out_specs=(both,) + weights,
        check_vma=False,
    )
```

```python
import functools
import jax
import jax.numpy as jnp
from jax import lax
from jax.experimental import pallas as pl
from jax.experimental.pallas import tpu as pltpu
from jax.sharding import PartitionSpec as P

F32 = jnp.float32
BF16 = jnp.bfloat16
I32 = jnp.int32
D = 768
FF = 2048
HEADS = 12
VOCAB = 256
BUCKETS = 32
TOK = 512
BYTES = 1024
PAD = 64
SPAN = BYTES + 2 * PAD
THRESHOLDS = (12, 16, 23, 32, 46, 64, 91)
EPSILON = 1e-06
MESH = pl.DeviceIdType.MESH


class Sizes:
    def __init__(self, shards):
        self.shards = shards
        self.emb = VOCAB // shards
        self.d = D // shards
        self.ff = FF // shards
        self.rel = BUCKETS * HEADS // shards


def nn(a, b):
    return jnp.dot(a, b, preferred_element_type=F32)


def nt(a, b):
    return lax.dot_general(a, b, (((1,), (1,)), ((), ())), preferred_element_type=F32)


def tn(a, b):
    return lax.dot_general(a, b, (((0,), (0,)), ((), ())), preferred_element_type=F32)


def iota(shape, dim):
    return lax.broadcasted_iota(I32, shape, dim)


def split3_rows(row):
    hi = row.astype(BF16).astype(F32)
    mid = (row - hi).astype(BF16).astype(F32)
    low = (row - hi - mid).astype(BF16).astype(F32)
    at = iota(row.shape, 0)
    zero = jnp.zeros_like(row)
    return jnp.where(at == 0, hi, jnp.where(at == 1, mid, jnp.where(at == 2, low, zero))).astype(BF16)


def expand_smalls(sz, small):
    wide = jnp.zeros((16, D), F32)
    flat = jnp.zeros((16, BUCKETS * HEADS), F32)
    for s in range(sz.shards):
        piece = small[s]
        i, c = iota((128, D), 0), iota((128, D), 1)
        place = jnp.where((c == i + s * sz.d) & (i < sz.d), 1.0, 0.0).astype(BF16)
        wide = wide + nn(piece, place)
        i, c = iota((128, BUCKETS * HEADS), 0), iota((128, BUCKETS * HEADS), 1)
        place = jnp.where((c == i + s * sz.rel) & (i < sz.rel), 1.0, 0.0).astype(BF16)
        flat = flat + nn(piece, place)
    return wide, flat


def bucket_of(relative):
    distance = jnp.abs(relative)
    far = jnp.full(relative.shape, 8, I32)
    for threshold in THRESHOLDS:
        far = far + jnp.where(distance >= threshold, 1, 0)
    return jnp.where(distance < 8, distance, far) + jnp.where(relative > 0, 16, 0)


def offset_buckets():
    return jnp.where(
        bucket_of(iota((128, 1024), 1) - 512) == iota((128, 1024), 0), 1.0, 0.0
    ).astype(BF16)


def offset_bias(flat):
    n = BUCKETS * HEADS
    row = jnp.broadcast_to(flat[8:9, :], (16, n))
    h, c = iota((16, n), 0), iota((16, n), 1)
    mine = jnp.where(lax.rem(c, HEADS) == h, row, 0.0).astype(BF16)
    c, b = iota((n, 128), 0), iota((n, 128), 1)
    by_bucket = nn(mine, jnp.where(lax.div(c, HEADS) == b, 1.0, 0.0).astype(BF16))
    return nn(by_bucket.astype(BF16), offset_buckets())


def toeplitz(row):
    wide = jnp.broadcast_to(row, (128, 1024))
    return pltpu.roll(wide, 0, 1, stride=1, stride_axis=0)[:, 128:1024]


def key_span(block):
    return max(0, block - 2) * 128, min(4, block + 3) * 128


def band(i, seg_q, seg_p):
    r, lane = iota((128, 256), 0), iota((128, 256), 1)
    p = 128 * i + 2 * (r & 63) + (r >> 6)
    q = 128 * i - PAD + lane
    same = jnp.concatenate([seg_p, seg_p], axis=0) == seg_q
    one = jnp.where(p == q, 1.0, 0.0)
    two = jnp.where((p >> 1) == (q >> 1), 0.5, 0.0)
    third_p, third_q = (p * 43691) >> 17, (q * 43691) >> 17
    three = jnp.where(same & (third_p == third_q), 1.0, 0.0)
    four = jnp.where(same & ((p >> 2) == (q >> 2)), 1.0, 0.0)
    three = three / jnp.sum(three, axis=1, keepdims=True)
    four = four / jnp.sum(four, axis=1, keepdims=True)
    return one, two, three, four


def band_weights(averages, u):
    scores = [jnp.sum(a * u, axis=1, keepdims=True) for a in averages]
    top = jnp.maximum(jnp.maximum(scores[0], scores[1]), jnp.maximum(scores[2], scores[3]))
    raised = [jnp.exp(s - top) for s in scores]
    total = raised[0] + raised[1] + raised[2] + raised[3]
    return [e / total for e in raised]


def segments(seg_ref, seg_col):
    marked = jnp.broadcast_to(seg_ref[0:1, :].astype(F32) + 1.0, (16, TOK))
    first = jnp.where(iota((16, TOK), 0) == 0, marked, 0.0).astype(BF16)
    seg_col[...] = tn(first, jnp.ones((16, 256), BF16))
    t, j = iota((TOK, SPAN), 0), iota((TOK, SPAN), 1)
    spread = jnp.where(((j - PAD) >> 1) == t, 1.0, 0.0).astype(BF16)
    return nn(marked.astype(BF16), spread)[0:8]


def byte_tables(ids_ref, seg_pad, table):
    ids = jnp.broadcast_to(ids_ref[0:1, :].astype(F32), (8, BYTES))
    ids = pltpu.roll(jnp.concatenate([ids, jnp.zeros((8, 2 * PAD), F32)], axis=1), PAD, 1)
    kept = jnp.full((16, SPAN), -1.0, F32)
    at = iota((16, SPAN), 0)
    for k in range(4):
        turn = (2 - k) % SPAN
        near = ids if turn == 0 else pltpu.roll(ids, turn, 1)
        near_seg = seg_pad if turn == 0 else pltpu.roll(seg_pad, turn, 1)
        row = jnp.where((near_seg == seg_pad) & (seg_pad > 0.5), near, -1.0)
        kept = jnp.where(at == k, jnp.concatenate([row, row], axis=0), kept)
    kept = kept.astype(BF16)
    pick = jnp.where(iota((16, 1024), 0) == (iota((16, 1024), 1) >> 8), 1.0, 0.0).astype(BF16)
    value = (iota((128, 1024), 1) & 255).astype(F32)
    for c in range(SPAN // 128):
        spread = tn(kept[:, 128 * c : 128 * c + 128], pick)
        table[128 * c : 128 * c + 128, :] = jnp.where(spread == value, 1.0, 0.0).astype(BF16)


def tap_table(embed, wide, t_hi, t_low):
    for k in range(4):
        product = embed * wide[k : k + 1, :]
        high = product.astype(BF16)
        t_hi[256 * k : 256 * k + 256, :] = high
        t_low[256 * k : 256 * k + 256, :] = (product - high.astype(F32)).astype(BF16)


def score_row(wide, t_hi, t_low, table):
    score = jnp.broadcast_to(wide[5:6, :], (16, D)).astype(BF16)
    by_tap = nt(score, t_hi[...]) + nt(score, t_low[...])
    u = jnp.sum(nt(split3_rows(by_tap), table[...]), axis=0, keepdims=True)
    return u + jnp.sum(wide[4:5, :] * wide[5:6, :], axis=1, keepdims=True)


def rms_rows(x, gain):
    scale = lax.rsqrt(jnp.mean(x * x, axis=1, keepdims=True) + EPSILON)
    return x * scale * gain


def rms_back(x, gain, dy):
    scale = lax.rsqrt(jnp.mean(x * x, axis=1, keepdims=True) + EPSILON)
    hat = x * scale
    dg = dy * gain
    inner = jnp.mean(dg * hat, axis=1, keepdims=True)
    return scale * (dg - hat * inner), dy * hat


def gelu_parts(x):
    c = 0.7978845608028654
    square = x * x
    t = jnp.tanh(c * x * (1.0 + 0.044715 * square))
    half = 0.5 * (1.0 + t)
    slope = half + 0.5 * x * (1.0 - t * t) * (c * (1.0 + 3 * 0.044715 * square))
    return x * half, slope


def lane_half(e):
    lanes = iota((1, 128), 1)
    return (lanes < 64) if e == 0 else (lanes >= 64)


def masked(x, e):
    return jnp.where(lane_half(e), x, jnp.zeros_like(x))


def forward_mix(seg_col, rows_ref, table, mix):
    @pl.loop(0, BYTES // 128)
    def _(i):
        window = pl.ds(pl.multiple_of(128 * i, 128), 256)
        tokens = pl.ds(pl.multiple_of(64 * i, 64), 64)
        averages = band(i, rows_ref[0:1, window], seg_col[tokens, :])
        weights = band_weights(averages, rows_ref[8:9, window])
        blend = sum(wt * a for wt, a in zip(weights, averages))
        pair = 0.5 * (blend[0:64] + blend[64:128])
        mix[tokens, :] = nn(pair.astype(BF16), table[pl.ds(pl.multiple_of(128 * i, 128), 256), :]).astype(BF16)


def forward_h0(mix, t_hi, wide, h0):
    for c in range(3):
        cols = slice(256 * c, 256 * c + 256)
        h0[:, cols] = nn(mix[...], t_hi[:, cols]) + wide[4:5, cols]


def norm_into(x_ref, gain, out_ref):
    @pl.loop(0, 4)
    def _(i):
        rows = pl.ds(pl.multiple_of(128 * i, 128), 128)
        out_ref[rows, :] = rms_rows(x_ref[rows, :], gain).astype(BF16)


def forward_projection(n, w4, attn_in, qkv):
    for c in range(3):
        cols = slice(256 * c, 256 * c + 256)
        qkv[n, :, cols] = nn(attn_in[...], w4[n, :, cols]).astype(BF16)


def forward_pair(hp, qkv, bias_ref, seg_col, rows_tok, probs, ctx):
    lanes = pl.ds(pl.multiple_of(128 * hp, 128), 128)
    keys = qkv[1, :, lanes]
    values = [masked(qkv[2, :, lanes], e) for e in (0, 1)]
    bias = [toeplitz(bias_ref[pl.ds(2 * hp + e, 1), :]) for e in (0, 1)]
    for block in range(4):
        lo, hi = key_span(block)
        rows = slice(128 * block, 128 * block + 128)
        q = qkv[0, rows, lanes]
        seg_p = seg_col[rows, 0:128]
        seg_p = jnp.concatenate([seg_p] * ((hi - lo) // 128), axis=1)
        seen = seg_p == rows_tok[0:1, lo:hi]
        out = jnp.zeros((128, 128), F32)
        for e in (0, 1):
            s = nt(masked(q, e), keys[lo:hi]) * 0.125
            at = (3 - block) * 128 + lo
            s = jnp.where(seen, s + bias[e][:, at : at + hi - lo], -1e9)
            s = jnp.exp(s - jnp.max(s, axis=1, keepdims=True))
            p = (s * (1.0 / jnp.sum(s, axis=1, keepdims=True))).astype(BF16)
            probs[2 * hp + e, rows, lo:hi] = p
            if hi - lo < TOK:
                gap = slice(384, 512) if block == 0 else slice(0, 128)
                probs[2 * hp + e, rows, gap] = jnp.zeros((128, 128), BF16)
            out = out + nn(p, values[e][lo:hi])
        ctx[rows, lanes] = out.astype(BF16)


def forward_out(w4, ctx, h0, h1):
    for c in range(3):
        cols = slice(256 * c, 256 * c + 256)
        h1[:, cols] = h0[:, cols] + nn(ctx[...], w4[3, :, cols])


def ffn_chunk(c, wgu, wd, ffn_in, dl, out, dx):
    units = pl.ds(pl.multiple_of(256 * c, 256), 256)
    uppers = pl.ds(pl.multiple_of(FF + 256 * c, 256), 256)
    gate = nn(ffn_in[...], wgu[:, units])
    up = nn(ffn_in[...], wgu[:, uppers])
    dh = nt(dl[...], wd[units, :])
    act, slope = gelu_parts(gate)
    hidden = (act * up).astype(BF16)
    dgate = (dh * (slope * up)).astype(BF16)
    dup = (dh * act).astype(BF16)
    for n in range(3):
        cols = slice(256 * n, 256 * n + 256)
        out[:, cols] += nn(hidden, wd[units, cols])
        dx[:, cols] += nt(dgate, wgu[cols, units]) + nt(dup, wgu[cols, uppers])
    wd[units, :] = tn(hidden, dl[...]).astype(BF16)
    wgu[:, units] = tn(ffn_in[...], dgate).astype(BF16)
    wgu[:, uppers] = tn(ffn_in[...], dup).astype(BF16)


def backward_norm(x_ref, gain, dy_ref, add, out_ref):
    def step(i, total):
        rows = pl.ds(pl.multiple_of(128 * i, 128), 128)
        dx, dgain = rms_back(x_ref[rows, :], gain, dy_ref[rows, :])
        out_ref[rows, :] = add[rows, :].astype(F32) + dx
        return total + jnp.sum(dgain, axis=0, keepdims=True)

    return lax.fori_loop(0, 4, step, jnp.zeros((1, D), F32))


def backward_out(w4, ctx, dh1, da, dctx):
    da[...] = dh1[...].astype(BF16)
    for c in range(3):
        cols = slice(256 * c, 256 * c + 256)
        dctx[:, cols] = nt(da[...], w4[3, cols, :]).astype(BF16)
    for c in range(3):
        cols = slice(256 * c, 256 * c + 256)
        w4[3, :, cols] = tn(ctx[...], da[:, cols]).astype(BF16)


def diagonal_sums(x):
    total = x[0:8, :]
    for a in range(1, 16):
        total = total + pltpu.roll(x[8 * a : 8 * a + 8, :], 1024 - 8 * a, 1)
    row = iota((8, 1024), 0)
    for bit in (1, 2, 4):
        total = jnp.where((row & bit) != 0, pltpu.roll(total, 1024 - bit, 1), total)
    return jnp.sum(total, axis=0, keepdims=True)


def backward_pair(hp, qkv, probs, ctx, dctx, dqkv, by_offset, ds_ref, bias_sum):
    lanes = pl.ds(pl.multiple_of(128 * hp, 128), 128)
    q, keys, values = (qkv[n, :, lanes] for n in range(3))
    dc = dctx[:, lanes]
    inner = dc.astype(F32) * ctx[:, lanes].astype(F32)
    dk = jnp.zeros((TOK, 128), F32)
    dv = jnp.zeros((TOK, 128), F32)
    for e in (0, 1):
        p_ref = probs.at[e]
        bias_sum[...] = jnp.zeros_like(bias_sum)
        for block in range(4):
            lo, hi = key_span(block)
            rows = slice(128 * block, 128 * block + 128)
            delta = jnp.sum(masked(inner[rows], e), axis=1, keepdims=True)
            dp = nt(masked(dc[rows], e), values[lo:hi])
            ds = p_ref[rows, lo:hi].astype(F32) * (dp - delta)
            at = (3 - block) * 128 + lo
            bias_sum[:, at : at + hi - lo] += ds
            ds_ref[e, rows, lo:hi] = ds.astype(BF16)
            if hi - lo < TOK:
                gap = slice(384, 512) if block == 0 else slice(0, 128)
                ds_ref[e, rows, gap] = jnp.zeros((128, 128), BF16)
        dv = dv + tn(p_ref[...], masked(dc, e))
        dk = dk + tn(ds_ref[e], masked(q, e))
        by_offset[pl.ds(2 * hp + e, 1), :] = diagonal_sums(bias_sum)
    dq = jnp.concatenate(
        [
            nn(ds_ref[0, 128 * b : 128 * b + 128, :], masked(keys, 0))
            + nn(ds_ref[1, 128 * b : 128 * b + 128, :], masked(keys, 1))
            for b in range(4)
        ],
        axis=0,
    )
    dqkv[0, :, lanes] = (dq * 0.125).astype(BF16)
    dqkv[1, :, lanes] = (dk * 0.125).astype(BF16)
    dqkv[2, :, lanes] = dv.astype(BF16)


def bias_gradient(by_offset):
    buckets = bucket_of(iota((128, 1024), 1) - 384)
    pick = jnp.where(buckets == iota((128, 1024), 0), 1.0, 0.0).astype(BF16)
    total = jnp.zeros((16, 128), F32)
    rest = by_offset
    for _ in range(3):
        part = rest.astype(BF16)
        total = total + nt(part, pick)
        rest = rest - part.astype(F32)
    n = BUCKETS * HEADS
    b, c = iota((128, n), 0), iota((128, n), 1)
    place = jnp.where(lax.div(c, HEADS) == b, 1.0, 0.0).astype(BF16)
    spread = jnp.zeros((16, n), F32)
    rest = total
    for _ in range(3):
        part = rest.astype(BF16)
        spread = spread + nn(part, place)
        rest = rest - part.astype(F32)
    h, c = iota((16, n), 0), iota((16, n), 1)
    return jnp.sum(jnp.where(lax.rem(c, HEADS) == h, spread, 0.0), axis=0, keepdims=True)


def backward_projection(n, first, w4, attn_in, dqkv, dx):
    for c in range(3):
        cols = slice(256 * c, 256 * c + 256)
        part = nt(dqkv[n], w4[n, cols, :])
        dx[:, cols] = part if first else dx[:, cols] + part
    for c in range(3):
        cols = slice(256 * c, 256 * c + 256)
        w4[n, :, cols] = tn(attn_in[...], dqkv[n, :, cols]).astype(BF16)


def backward_near(t_hi, dh0, dh0_low, q_ref):
    dh0_low[...] = dh0[...].astype(BF16)
    for c in range(4):
        at = 256 * (c % 2)
        q_ref[c // 2, :, at : at + 256] = nt(dh0_low[...], t_hi[256 * c : 256 * c + 256, :]).astype(BF16)


def backward_mix(wide, seg_col, rows_ref, table, dh0, q_ref, du_ref):
    du_ref[...] = jnp.zeros_like(du_ref)

    @pl.loop(0, BYTES // 128)
    def _(i):
        window = pl.ds(pl.multiple_of(128 * i, 128), 256)
        tokens = pl.ds(pl.multiple_of(64 * i, 64), 64)
        averages = band(i, rows_ref[0:1, window], seg_col[tokens, :])
        weights = band_weights(averages, rows_ref[8:9, window])
        near = jnp.sum(dh0[tokens, :] * wide[4:5, :], axis=1, keepdims=True)
        for n in range(2):
            near = near + nt(q_ref[n, tokens, :], table[window, 512 * n : 512 * n + 512])
        near = jnp.concatenate([near, near], axis=0) * 0.5
        dws = [jnp.sum(a * near, axis=1, keepdims=True) for a in averages]
        mean = sum(wt * dw for wt, dw in zip(weights, dws))
        total = sum((wt * (dw - mean)) * a for wt, dw, a in zip(weights, dws, averages))
        du_ref[0:1, window] += jnp.sum(total, axis=0, keepdims=True)


def backward_taps(we, wide, table, t_hi, t_low, mix, dh0, dh0_low, du_ref):
    du = du_ref[0:1, :]
    du_sum = jnp.sum(du, axis=1, keepdims=True)
    by_tap = jnp.sum(nn(split3_rows(jnp.broadcast_to(du, (16, SPAN))), table[...]), axis=0, keepdims=True)
    parts = split3_rows(jnp.broadcast_to(by_tap, (16, 1024)))
    score = jnp.broadcast_to(wide[5:6, :], (16, D)).astype(BF16)
    dscore = jnp.sum(nn(parts, t_hi[...]) + nn(parts, t_low[...]), axis=0, keepdims=True) + du_sum * wide[4:5, :]
    dconv_b = jnp.sum(dh0[...], axis=0, keepdims=True) + du_sum * wide[5:6, :]
    dconv = [[] for _ in range(4)]
    for c in range(3):
        cols = slice(256 * c, 256 * c + 256)
        embed = we[:, cols].astype(F32)
        dembed = jnp.zeros((VOCAB, 256), F32)
        for k in range(4):
            rows = slice(256 * k, 256 * k + 256)
            dt = tn(mix[:, rows], dh0_low[:, cols]) + tn(parts[:, rows], score[:, cols])
            dembed = dembed + dt * wide[k : k + 1, cols]
            dconv[k].append(jnp.sum(dt * embed, axis=0, keepdims=True))
        we[:, cols] = dembed.astype(BF16)
    return [jnp.concatenate(d, axis=1) for d in dconv], dconv_b, dscore


def pack_smalls(sz, rows, flat, out):
    at = iota((16, D), 0)
    wide = jnp.zeros((16, D), F32)
    for n, row in enumerate(rows):
        wide = jnp.where(at == n, jnp.broadcast_to(row, (16, D)), wide)
    wide = wide.astype(BF16)
    n = BUCKETS * HEADS
    rel = jnp.where(iota((16, n), 0) == 8, jnp.broadcast_to(flat, (16, n)), 0.0).astype(BF16)
    for s in range(sz.shards):
        c, i = iota((D, 128), 0), iota((D, 128), 1)
        place = jnp.where((c == i + s * sz.d) & (i < sz.d), 1.0, 0.0).astype(BF16)
        c, i = iota((n, 128), 0), iota((n, 128), 1)
        place_rel = jnp.where((c == i + s * sz.rel) & (i < sz.rel), 1.0, 0.0).astype(BF16)
        out[s] = (nn(wide, place) + nn(rel, place_rel)).astype(BF16)


REDUCE_ORDER = ("g0", "g1", "d0", "g2", "g3", "d1", "o", "v", "k", "q", "e")
LONE = {"e": 0, "q": 128, "k": 128, "v": 128, "o": 128, "d0": 128, "g0": 256, "g1": 128, "d1": 128, "g2": 128, "g3": 0}
REDUCE_LONE = {"e": 0, "q": 128, "k": 128, "v": 128, "o": 128, "d0": 128, "g0": 128, "g1": 128, "d1": 128, "g2": 128, "g3": 256}
OUTER_FIRST = ()
PLAN = {
    "start": ("Zm", "Ze", "Zq", "Zk", "Zv", "Zo",),
    "cast4": ("Zd0", "Ym",),
    "cast5": ("Ye",),
    "t2": ("Yq", "Xe", "Ce",),
    "t3": ("Yk",),
    "t4": ("Xq", "Yv", "Zg0",),
    "t5": ("Xk", "Zg1", "Yo", "Cq", "Xv",),
    "p0": ("Zd1", "Yd0", "Ck", "Xo",),
    "p1": ("Yg0", "Cv", "Zg2",),
    "p2": ("Xd0", "Co",),
    "a0": ("Yg1", "Zg3", "Xg0",),
    "a2": ("Cd0", "Yd1",),
    "a3": ("Xg1",),
    "a4": ("Yg2",),
    "a5": ("Cg0", "Xd1",),
    "f0": ("Cg1",),
    "f1": ("Xg2", "Yg3", "cg0",),
    "f2": ("Cd1", "xg0",),
    "f3": ("cg1", "cd0", "Cg2", "xg1", "xd0",),
    "f4": ("Xg3", "Cg3", "yg0",),
    "f5": ("yg1", "cg2",),
    "f6": ("xg2",),
    "f7": ("yd0", "cg3", "zg0", "cd1",),
    "g0": ("xg3",),
    "g1": ("yg2", "xd1", "co",),
    "b0": ("zg1", "xo",),
    "b1": ("lg0",),
    "b3": ("zd0", "yg3",),
    "b4": ("lg1",),
    "q2": ("zg2", "yd1", "cv",),
    "q1": ("ld0", "xv", "ck",),
    "q0": ("zg3", "yo", "sg0", "xk", "cq",),
    "g2": ("wg0", "sg1",),
    "g3": ("wg1", "sd0", "lg2", "zd1", "wd0", "xq",),
    "g4": ("lg3", "zo", "yv",),
    "g5": ("ce",),
    "g6": ("yk", "xe", "ye", "sg2", "ld1", "cm", "wg2", "xm", "zv",),
    "end": ("lo", "yq", "sg3", "zk", "wg3", "sd1", "so", "wd1", "ze", "lv", "wo", "zm", "sv", "lk", "zq", "wv", "le", "lm", "sk", "wk", "se", "sm", "we", "lq", "sq", "wq",),
}


class Place:
    def __init__(self, shards, copies):
        self.shards, self.copies = shards, copies
        self.inner = 2 if shards < 16 else 4
        self.outer = shards // self.inner
        self.planes = copies // 2
        f, d = lax.axis_index("fsdp"), lax.axis_index("dp")
        self.f, self.d = f, d
        self.f1, self.f2 = lax.div(f, self.inner), lax.rem(f, self.inner)
        self.x, self.core = lax.div(d, 2), lax.rem(d, 2)

    def shard(self, k, i):
        f1 = lax.rem(self.f1 + (self.outer - k), self.outer)
        f2 = lax.rem(self.f2 + (self.inner - i), self.inner)
        return f1 * self.inner + f2

    def outer_peer(self, k):
        return (lax.rem(self.f1 + k, self.outer) * self.inner + self.f2, self.d)

    def inner_peer(self, i):
        return (self.f1 * self.inner + lax.rem(self.f2 + i, self.inner), self.d)

    def plane_peer(self, p):
        return (self.f, lax.rem(self.x + p, self.planes) * 2 + self.core)

    def sibling(self):
        return (self.f, self.x * 2 + (1 - self.core))

    def peers(self):
        found = [self.outer_peer(k) for k in range(1, self.outer)]
        found += [self.inner_peer(i) for i in range(1, self.inner)]
        found += [self.plane_peer(p) for p in range(1, self.planes)]
        return found + [self.sibling()]

    def greet(self):
        for peer in self.peers():
            pl.semaphore_signal(pltpu.get_barrier_semaphore(), inc=1, device_id=peer, device_id_type=MESH)

    def await_greetings(self):
        pl.semaphore_wait(pltpu.get_barrier_semaphore(), len(self.peers()))


def aligned(value, unit):
    return value if isinstance(value, int) else pl.multiple_of(value, unit)


def remote(src, dst, send, recv, peer):
    return pltpu.make_async_remote_copy(
        src_ref=src, dst_ref=dst, send_sem=send, recv_sem=recv, device_id=peer, device_id_type=MESH
    )


class Part:
    def __init__(self, first, rows, base, gap, half, lone):
        self.first, self.rows = first, rows
        self.base, self.gap, self.half, self.lone = base, gap, half, lone

    def split(self, place):
        return self.lone if place.planes == 2 else 0

    def wide(self, place):
        return self.half - self.split(place)

    def view(self, ref, shard, column, width):
        row = aligned(shard * self.rows + self.first, 16)
        return ref.at[pl.ds(row, self.rows), pl.ds(aligned(column, 128), width)]

    def every(self, ref, place, column, width):
        return ref.at[pl.ds(self.first, place.shards * self.rows), pl.ds(aligned(column, 128), width)]

    def column(self, ref, place, f2, start, width):
        block = ref.at[pl.ds(self.first, place.shards * self.rows), :]
        block = block.reshape(place.outer, place.inner * self.rows, block.shape[1])
        row = aligned(f2 * self.rows, 16)
        return block.at[:, pl.ds(row, self.rows), pl.ds(aligned(start, 128), width)]

    def start(self, place):
        return place.core * self.gap + self.base

    def start_other(self, place):
        return (1 - place.core) * self.gap + self.base

    def mine(self, ref, place, shard):
        return self.view(ref, shard, self.start(place) + place.x * self.split(place), self.wide(place))

    def moved(self, ref, place, f2):
        return self.column(ref, place, f2, self.start(place) + place.x * self.split(place), self.wide(place))

    def kept(self, ref, place):
        return self.every(ref, place, self.start(place) + place.x * self.wide(place), self.lone)

    def lacked(self, ref, place):
        return self.every(ref, place, self.start(place) + (1 - place.x) * self.wide(place), self.lone)


class Sends:
    def _start(self, n, src, dst, peer):
        def make():
            return remote(src(), dst(), self.send.at[n], self.recv.at[n], peer())

        make().start()
        self.sent.append(make)

    def _await(self, n, dst, peer):
        remote(dst, dst, self.send.at[n], self.recv.at[n], peer).wait_recv()

    def finish(self):
        for make in self.sent:
            make().wait_send()


class Gather(Sends):
    @staticmethod
    def sems(shards):
        inner = 2 if shards < 16 else 4
        return shards // inner + inner

    def __init__(self, place, part, ref, send, recv):
        self.place, self.part, self.ref = place, part, ref
        self.send, self.recv = send, recv
        self.sent = []

    def first(self):
        place = self.place

        def own():
            return self.part.mine(self.ref, place, place.f)

        for k in range(1, place.outer):
            self._start(k - 1, own, own, functools.partial(place.outer_peer, k))

    def second(self):
        place = self.place
        for k in range(1, place.outer):
            self._await(k - 1, self.part.mine(self.ref, place, place.shard(k, 0)), place.outer_peer(k))

        def column():
            return self.part.moved(self.ref, place, place.f2)

        for i in range(1, place.inner):
            self._start(place.outer + i - 2, column, column, functools.partial(place.inner_peer, i))

    def third(self):
        place, part = self.place, self.part
        for i in range(1, place.inner):
            f2 = lax.rem(place.f2 + (place.inner - i), place.inner)
            self._await(place.outer + i - 2, part.moved(self.ref, place, f2), place.inner_peer(i))
        if part.split(place):

            def kept():
                return part.kept(self.ref, place)

            self._start(place.outer + place.inner - 2, kept, kept, functools.partial(place.plane_peer, 1))

    def fourth(self):
        place, part = self.place, self.part
        if part.split(place):
            self._await(place.outer + place.inner - 2, part.lacked(self.ref, place), place.plane_peer(1))

        def half():
            return part.every(self.ref, place, part.start(place), part.half)

        self._start(place.outer + place.inner - 1, half, half, place.sibling)

    def fifth(self):
        place, part = self.place, self.part
        view = part.every(self.ref, place, part.start_other(place), part.half)
        self._await(place.outer + place.inner - 1, view, place.sibling())


def add_rows(target, source, rows, step):
    if rows <= step:
        target[...] = (target[...].astype(F32) + source[...].astype(F32)).astype(BF16)
        return

    @pl.loop(0, rows // step)
    def _(n):
        at = pl.ds(pl.multiple_of(n * step, step), step)
        target[at, :] = (target[at, :].astype(F32) + source[at, :].astype(F32)).astype(BF16)


class Reduce(Sends):
    @staticmethod
    def buffers(shards, copies, part, outer_first):
        inner = 2 if shards < 16 else 4
        outer = shards // inner
        planes = copies // 2
        split = part.lone if planes == 2 else 0
        wide = part.half - split
        if outer_first:
            across = [(inner - 1, part.rows, wide), (outer - 1, inner * part.rows, wide)]
        else:
            across = [(inner - 1, outer, part.rows, wide), (outer - 1, part.rows, wide)]
        shapes = [
            (shards * part.rows, part.half),
            (shards * part.rows, split) if split else (16, 128),
            *across,
            (planes - 1, part.rows, wide),
        ]
        return [pltpu.VMEM(s, BF16) for s in shapes]

    @staticmethod
    def sems(shards, copies):
        inner = 2 if shards < 16 else 4
        return shards // inner + inner + copies // 2

    def __init__(self, place, part, ref, out, bufs, send, recv, outer_first):
        self.outer_first = outer_first
        self.place, self.part, self.ref, self.out = place, part, ref, out
        self.from_core, self.from_plane, self.from_inner, self.from_outer, self.last = bufs
        self.send, self.recv = send, recv
        self.sent = []
        self.rows = place.shards * part.rows

    def _columns(self, column, width):
        return self.part.every(self.ref, self.place, column, width)

    def first(self):
        place, part = self.place, self.part
        self._start(
            0,
            lambda: self._columns(part.start_other(place), part.half),
            lambda: self.from_core,
            place.sibling,
        )

    def second(self):
        place, part = self.place, self.part
        self._await(0, self.from_core, place.sibling())
        target = self._columns(part.start(place), part.half)
        add_rows(target, self.from_core, self.rows, 64)
        if part.split(place):
            self._start(
                1,
                lambda: self._columns(part.start(place) + (1 - place.x) * part.wide(place), part.lone),
                lambda: self.from_plane,
                functools.partial(place.plane_peer, 1),
            )
        else:
            self._across()

    def _block(self, k):
        place, part = self.place, self.part
        rows = place.inner * part.rows
        row = aligned(lax.rem(place.f1 + k, place.outer) * rows + part.first, 16)
        column = aligned(part.start(place) + place.x * part.split(place), 128)
        return self.ref.at[pl.ds(row, rows), pl.ds(column, part.wide(place))]

    def _across(self):
        place, part = self.place, self.part
        if self.outer_first:
            for k in range(1, place.outer):
                self._start(
                    place.inner + k,
                    functools.partial(self._block, k),
                    lambda k=k: self.from_outer.at[k - 1],
                    functools.partial(place.outer_peer, k),
                )
            return
        for i in range(1, place.inner):
            self._start(
                1 + i,
                lambda i=i: part.moved(self.ref, place, lax.rem(place.f2 + i, place.inner)),
                lambda i=i: self.from_inner.at[i - 1],
                functools.partial(place.inner_peer, i),
            )

    def third(self):
        place, part = self.place, self.part
        if part.split(place):
            self._await(1, self.from_plane, place.plane_peer(1))
            target = self._columns(part.start(place) + place.x * part.wide(place), part.lone)
            add_rows(target, self.from_plane, self.rows, 128)
            self._across()

    def fourth(self):
        place, part = self.place, self.part
        if self.outer_first:
            for k in range(1, place.outer):
                self._await(place.inner + k, self.from_outer.at[k - 1], place.outer_peer(k))
            block = self._block(0)
            total = block[...].astype(F32)
            for k in range(1, place.outer):
                total = total + self.from_outer[k - 1].astype(F32)
            block[...] = total.astype(BF16)
            for i in range(1, place.inner):

                def theirs(i=i):
                    f2 = lax.rem(place.f2 + i, place.inner)
                    return part.mine(self.ref, place, place.f1 * place.inner + f2)

                self._start(
                    1 + i, theirs, lambda i=i: self.from_inner.at[i - 1], functools.partial(place.inner_peer, i)
                )
            return
        for i in range(1, place.inner):
            self._await(1 + i, self.from_inner.at[i - 1], place.inner_peer(i))
        for k in list(range(1, place.outer)) + [0]:

            def mine(k=k):
                f1 = lax.rem(place.f1 + k, place.outer)
                return part.mine(self.ref, place, f1 * place.inner + place.f2)

            target = mine()
            total = target[...].astype(F32)
            for i in range(1, place.inner):
                total = total + self.from_inner[i - 1, lax.rem(place.f1 + k, place.outer)].astype(F32)
            target[...] = total.astype(BF16)
            if k:
                self._start(
                    place.inner + k,
                    mine,
                    functools.partial(lambda k: self.from_outer.at[k - 1], k),
                    functools.partial(place.outer_peer, k),
                )

    def fifth(self):
        place, part = self.place, self.part
        target = part.mine(self.ref, place, place.f)
        if self.outer_first:
            for i in range(1, place.inner):
                self._await(1 + i, self.from_inner.at[i - 1], place.inner_peer(i))
            total = target[...].astype(F32)
            for i in range(1, place.inner):
                total = total + self.from_inner[i - 1].astype(F32)
        else:
            for k in range(1, place.outer):
                self._await(place.inner + k, self.from_outer.at[k - 1], place.outer_peer(k))
            total = target[...].astype(F32)
            for k in range(1, place.outer):
                total = total + self.from_outer[k - 1].astype(F32)
        target[...] = total.astype(BF16)
        for p in range(1, place.planes):
            self._start(
                place.inner + place.outer - 1 + p,
                lambda: part.mine(self.ref, place, place.f),
                functools.partial(lambda p: self.last.at[p - 1], p),
                functools.partial(place.plane_peer, p),
            )

    def sixth(self):
        place, part = self.place, self.part
        for p in range(1, place.planes):
            self._await(place.inner + place.outer - 1 + p, self.last.at[p - 1], place.plane_peer(p))
        mine = part.mine(self.ref, place, place.f)[...].astype(F32)
        start = part.start(place)

        def put(column, width, values):
            self.out[:, pl.ds(aligned(start + column, 128), width)] = values.astype(BF16)

        if part.split(place):
            theirs = self.last[0].astype(F32)
            lone, wide, both = part.lone, part.wide(place), part.half - 2 * part.lone
            low = place.x == 0
            if both:
                shared = jnp.where(low, mine[:, lone:], mine[:, :both]) + jnp.where(low, theirs[:, :both], theirs[:, lone:])
                put(lone, both, shared)
            put(0, lone, jnp.where(low, mine[:, 0:lone], theirs[:, 0:lone]))
            put(wide, lone, jnp.where(low, theirs[:, both:], mine[:, both:]))
        else:
            for p in range(1, place.planes):
                mine = mine + self.last[p - 1].astype(F32)
            put(0, part.half, mine)
        n = place.inner + place.outer + place.planes - 1

        def whole():
            return self.out.at[:, pl.ds(aligned(part.start(place), 128), part.half)]

        self._start(n, whole, whole, place.sibling)

    def seventh(self):
        place, part = self.place, self.part
        view = self.out.at[:, pl.ds(aligned(part.start_other(place), 128), part.half)]
        self._await(place.inner + place.outer + place.planes - 1, view, place.sibling())


class SmallGather(Sends):
    @staticmethod
    def sems(shards):
        inner = 2 if shards < 16 else 4
        return shards // inner + inner - 2

    def __init__(self, place, small, send, recv):
        self.place, self.small, self.send, self.recv = place, small, send, recv
        self.sent = []

    def _column(self, f2):
        place = self.place
        return self.small.reshape(place.outer, place.inner * 16, 128).at[:, pl.ds(aligned(f2 * 16, 16), 16), :]

    def first(self):
        place = self.place

        def own():
            return self.small.at[place.f]

        for k in range(1, place.outer):
            self._start(k - 1, own, own, functools.partial(place.outer_peer, k))

    def second(self):
        place = self.place
        for k in range(1, place.outer):
            self._await(k - 1, self.small.at[place.shard(k, 0)], place.outer_peer(k))

        def column():
            return self._column(place.f2)

        for i in range(1, place.inner):
            self._start(place.outer + i - 2, column, column, functools.partial(place.inner_peer, i))

    def fifth(self):
        place = self.place
        for i in range(1, place.inner):
            f2 = lax.rem(place.f2 + (place.inner - i), place.inner)
            self._await(place.outer + i - 2, self._column(f2), place.inner_peer(i))


class SmallReduce(Sends):
    @staticmethod
    def sems(shards, copies):
        inner = 2 if shards < 16 else 4
        return shards // inner + inner + copies // 2 - 2

    @staticmethod
    def buffers(shards, copies):
        inner = 2 if shards < 16 else 4
        outer, planes = shards // inner, copies // 2
        shapes = [(shards, 16, 128), (inner - 1, outer, 16, 128), (outer - 1, 16, 128), (planes - 1, 16, 128)]
        return [pltpu.VMEM(s, BF16) for s in shapes]

    def __init__(self, place, gs, out, bufs, send, recv):
        self.place, self.gs, self.out, self.send, self.recv = place, gs, out, send, recv
        self.from_core, self.from_inner, self.from_outer, self.last = bufs
        self.sent = []

    def first(self):
        self._start(0, lambda: self.gs, lambda: self.from_core, self.place.sibling)

    def second(self):
        place = self.place
        self._await(0, self.from_core, place.sibling())
        self.sent.pop()().wait_send()
        self.gs[...] = (self.gs[...].astype(F32) + self.from_core[...].astype(F32)).astype(BF16)

        def column(i):
            f2 = lax.rem(place.f2 + i, place.inner)
            return self.gs.reshape(place.outer, place.inner * 16, 128).at[:, pl.ds(aligned(f2 * 16, 16), 16), :]

        for i in range(1, place.inner):
            self._start(
                i,
                functools.partial(column, i),
                lambda i=i: self.from_inner.at[i - 1],
                functools.partial(place.inner_peer, i),
            )

    def _tile(self, k):
        place = self.place
        return self.gs.at[lax.rem(place.f1 + k, place.outer) * place.inner + place.f2]

    def fourth(self):
        place = self.place
        for i in range(1, place.inner):
            self._await(i, self.from_inner.at[i - 1], place.inner_peer(i))
        for k in list(range(1, place.outer)) + [0]:
            total = self._tile(k)[...].astype(F32)
            for i in range(1, place.inner):
                total = total + self.from_inner[i - 1, lax.rem(place.f1 + k, place.outer)].astype(F32)
            self._tile(k)[...] = total.astype(BF16)
            if k:
                self._start(
                    place.inner - 1 + k,
                    functools.partial(self._tile, k),
                    lambda k=k: self.from_outer.at[k - 1],
                    functools.partial(place.outer_peer, k),
                )

    def fifth(self):
        place = self.place
        total = self._tile(0)[...].astype(F32)
        for k in range(1, place.outer):
            self._await(place.inner - 1 + k, self.from_outer.at[k - 1], place.outer_peer(k))
            total = total + self.from_outer[k - 1].astype(F32)
        self._tile(0)[...] = total.astype(BF16)
        for p in range(1, place.planes):
            self._start(
                place.inner + place.outer - 2 + p,
                functools.partial(self._tile, 0),
                lambda p=p: self.last.at[p - 1],
                functools.partial(place.plane_peer, p),
            )

    def sixth(self):
        place = self.place
        total = self._tile(0)[...].astype(F32)
        for p in range(1, place.planes):
            self._await(place.inner + place.outer - 2 + p, self.last.at[p - 1], place.plane_peer(p))
            total = total + self.last[p - 1].astype(F32)
        self.out[...] = total


VMEM_LIMIT = 64 * 1024 * 1024 - 65536


def gather_parts(sz, lone=LONE):
    parts = {"e": ("we", None, Part(0, sz.emb, 0, 384, 384, lone["e"]))}
    for n, name in enumerate("qkvo"):
        parts[name] = ("w4", n, Part(0, sz.d, 0, 384, 384, lone[name]))
    blocks = sz.ff // 128
    for j in range(4):
        if j % (4 // blocks) == 0:
            first = 128 * sz.shards * (j * blocks // 4)
            name = "d%d" % (j * blocks // 4)
            parts[name] = ("wd", None, Part(first, 128, 0, 384, 384, lone[name]))
        name = "g%d" % j
        parts[name] = ("wgu", None, Part(0, sz.d, 512 * j, FF, 512, lone[name]))
    return parts


def reduce_parts(sz):
    parts = gather_parts(sz, REDUCE_LONE)
    return {name: parts[name] for name in REDUCE_ORDER if name in parts}


class Schedule:
    def __init__(self, gathers, reduces, plan):
        self.jobs = {"G": gathers, "R": reduces}
        self.plan = plan
        self.done = []

    def go(self, step):
        kind, name = step[0], step[1:]
        gather = kind.isupper()
        job = self.jobs["G" if gather else "R"][name]
        step_of = {
            "Z": "first", "Y": "second", "X": "third", "C": "fourth", "W": "fifth", "F": "finish",
            "c": "first", "x": "second", "y": "third", "z": "fourth", "l": "fifth", "s": "sixth", "w": "seventh",
        }
        if step in self.done:
            return
        order = "ZYXCWF" if gather else "cxyzlsw"
        before = order[: order.index(kind)]
        missing = [b for b in before if hasattr(job, step_of[b]) and b + name not in self.done]
        for b in missing:
            self.go(b + name)
        if hasattr(job, step_of[kind]):
            getattr(job, step_of[kind])()
        self.done.append(step)

    def hook(self, name):
        for step in self.plan.get(name, ()):
            if step[1:] in self.jobs["G" if step[0].isupper() else "R"]:
                self.go(step)

    def need(self, *steps):
        for step in steps:
            self.go(step)

    def rest(self):
        for kind in "cxyzlsw":
            for name in self.jobs["R"]:
                self.go(kind + name)
        for job in list(self.jobs["R"].values()):
            job.finish()


def step_kernel(sz, copies, *refs):
    (ids, seg, embed, conv_w, conv_b, score_w, norm_attn, w_q, w_k, w_v, w_o, rel, norm_ffn, w_g, w_u, w_d, dl_h) = refs[:17]
    mixed_o, re_o, r4_o, rgu_o, rd_o, tile_o = refs[17:23]
    refs = refs[23:]
    (we, w4, wgu, wd, re, r4, rgu, rd, tile, small, gs, stage_small) = refs[:12]
    refs = refs[12:]
    (attn_in, qkv, probs, ctx, h0, h1, ffn_in, table, t_hi, t_low, mix, rows_ref, seg_col, wide_ref) = refs[:14]
    (bias_ref, mixed, dl, dx, dh1, dctx, da, ds_ref, bias_sum, by_off, du_ref) = refs[14:25]
    in_sems, out_sems, send, recv, r_send, r_recv, small_send, small_recv, sr_send, sr_recv = refs[25:35]
    buffers = refs[35:]
    place = Place(sz.shards, copies)
    place.greet()
    f = place.f
    arrays = dict(we=we, w4=w4, wgu=wgu, wd=wd)

    gathers = {"m": SmallGather(place, small, small_send, small_recv)}
    for n, (job, (name, lead, part)) in enumerate(gather_parts(sz).items()):
        ref = arrays[name] if lead is None else arrays[name].at[lead]
        gathers[job] = Gather(place, part, ref, send.at[n], recv.at[n])
    reduces = {}
    for n, (job, (name, lead, part)) in enumerate(reduce_parts(sz).items()):
        ref = arrays[name] if lead is None else arrays[name].at[lead]
        if name == "wd":
            block = part.first // (128 * sz.shards)
            out = rd.at[128 * block : 128 * block + 128, :]
        else:
            out = dict(we=re, w4=r4, wgu=rgu)[name]
            out = out if lead is None else out.at[lead]
        reduces[job] = Reduce(place, part, ref, out, buffers[5 * n : 5 * n + 5], r_send.at[n], r_recv.at[n], job in OUTER_FIRST)
    reduces["m"] = SmallReduce(place, gs, tile, buffers[5 * len(reduces) :], sr_send, sr_recv)
    sched = Schedule(gathers, reduces, PLAN)
    hook, need = sched.hook, sched.need

    mine = pl.ds(pl.multiple_of(place.core * 384, 128), 384)
    loads = []
    row = 0
    for n, (w, count) in enumerate(
        ((embed, sz.emb), (w_q, sz.d), (w_k, sz.d), (w_v, sz.d), (w_o, sz.d), (w_d, sz.ff))
    ):
        if n == 5:
            staged = dx.at[0:count, 384:768]
        else:
            staged = dx.at[row : row + count, 0:384]
        copy = pltpu.make_async_copy(w.at[:, mine], staged, in_sems.at[n])
        copy.start()
        loads.append((copy, staged))
        row += count

    def gu_copies(w):
        found = []
        for n in range(3):
            width = min(D, FF - n * D)
            staged = dh1.at[n * sz.d : n * sz.d + sz.d, 0:width]
            found.append(pltpu.make_async_copy(w.at[:, n * D : n * D + width], staged, in_sems.at[8 + n]))
        return found

    for core, w in enumerate((w_g, w_u)):

        @pl.when(place.core == core)
        def _(w=w):
            for copy in gu_copies(w):
                copy.start()

    dl_copy = pltpu.make_async_copy(dl_h, dl, in_sems.at[7])
    dl_copy.start()

    def own(rows, first=0):
        return pl.ds(pl.multiple_of(first + f * rows, 16), rows)

    def cast(n, name, target):
        copy, staged = loads[n]
        copy.wait()
        target[...] = staged[:, moved(name, 0)].astype(BF16)

    stage_small[...] = jnp.zeros_like(stage_small)
    stage_small[0:4, 0 : sz.d] = conv_w[...]
    for n, vector in enumerate((conv_b, score_w, norm_attn, norm_ffn)):
        stage_small[4 + n : 5 + n, 0 : sz.d] = vector[...].reshape(1, sz.d)
    stage_small[8:9, 0 : sz.rel] = rel[...].reshape(1, sz.rel)
    small[f] = stage_small[...].astype(BF16)

    def moved(name, start):
        split = LONE[name] if place.planes == 2 else 0
        return pl.ds(aligned(start + place.x * split, 128), 384 - split)

    cast(0, "e", we.at[own(sz.emb), moved("e", place.core * 384)])
    for n in range(4):
        cast(n + 1, "qkvo"[n], w4.at[n, own(sz.d), moved("qkvo"[n], place.core * 384)])
    place.await_greetings()
    hook("start")
    copy, staged = loads[5]
    copy.wait()
    for j in range(sz.ff // 128):
        rows = own(128, j * 128 * sz.shards)
        name = "d%d" % j
        wd[rows, moved(name, place.core * 384)] = staged[128 * j : 128 * j + 128, moved(name, 0)].astype(BF16)
    hook("cast4")
    for copy in gu_copies(w_g):
        copy.wait()
    blocks = sz.ff // 128
    for j in range(blocks):
        for s in range(sz.shards):
            n, at = divmod(s * sz.ff + 128 * j, D)
            column = 128 * (j * sz.shards + s)
            lone = LONE["g%d" % (column // 512)] if place.planes == 2 else 0

            def put(n=n, at=at, column=place.core * FF + column):
                values = dh1[n * sz.d : n * sz.d + sz.d, at : at + 128].astype(BF16)
                wgu[own(sz.d), pl.ds(pl.multiple_of(column, 128), 128)] = values

            if column % 512 < lone:
                pl.when(place.x == 0)(put)
            elif column % 512 >= 512 - lone:
                pl.when(place.x == 1)(put)
            else:
                put()
    hook("cast5")

    seg_pad = segments(seg, seg_col)
    hook("t0")
    byte_tables(ids, seg_pad, table)
    hook("t1")
    need("Wm")
    wide, flat = expand_smalls(sz, small)
    wide_ref[...] = wide
    bias_ref[...] = offset_bias(flat)
    hook("t2")
    need("We")
    tap_table(we[...].astype(F32), wide, t_hi, t_low)
    rows_ref[0:8, :] = seg_pad
    rows_ref[8:16, :] = jnp.broadcast_to(score_row(wide, t_hi, t_low, table), (8, SPAN))
    hook("t3")
    forward_mix(seg_col, rows_ref, table, mix)
    hook("t4")
    forward_h0(mix, t_hi, wide, h0)
    norm_into(h0, wide_ref[6:7, :], attn_in)
    hook("t5")
    for n in range(3):
        need("W" + "qkv"[n])
        forward_projection(n, w4, attn_in, qkv)
        hook("p%d" % n)
    rows_tok = seg[0:1, :].astype(F32) + 1.0

    @pl.loop(0, 6)
    def _(hp):
        forward_pair(hp, qkv, bias_ref, seg_col, rows_tok, probs, ctx)
        for n in range(6):
            if PLAN.get("a%d" % n):
                pl.when(hp == n)(functools.partial(hook, "a%d" % n))

    need("Wo")
    forward_out(w4, ctx, h0, h1)
    norm_into(h1, wide_ref[7:8, :], ffn_in)
    dh1[...] = h1[...]
    dx[...] = jnp.zeros_like(dx)
    dl_copy.wait()
    hook("o")

    for j in range(4):
        need("Wd%d" % (j * blocks // 4), "Wg%d" % j)
        if j % (4 // blocks) == 0:
            need("Fd%d" % (j * blocks // 4))
        need("Fg%d" % j)
        for c in (2 * j, 2 * j + 1):
            ffn_chunk(c, wgu, wd, ffn_in, dl, dh1, dx)
            hook("f%d" % c)
    mixed[...] = dh1[...].astype(BF16)
    mixed_copy = pltpu.make_async_copy(mixed, mixed_o, out_sems.at[0])
    mixed_copy.start()

    dnorm_ffn = backward_norm(h1, wide_ref[7:8, :], dx, dl, dh1)
    hook("g0")
    need("Fo")
    backward_out(w4, ctx, dh1, da, dctx)
    hook("g1")
    by_off[...] = jnp.zeros_like(by_off)
    bias_sum[...] = jnp.zeros_like(bias_sum)

    @pl.loop(0, 6)
    def _(hp):
        backward_pair(hp, qkv, probs.at[pl.ds(2 * hp, 2)], ctx, dctx, qkv, by_off, ds_ref, bias_sum)
        for n in range(6):
            if PLAN.get("b%d" % n):
                pl.when(hp == n)(functools.partial(hook, "b%d" % n))

    for n in (2, 1, 0):
        need("F" + "qkv"[n])
        backward_projection(n, n == 2, w4, attn_in, qkv, dx)
        hook("q%d" % n)
    dnorm_attn = backward_norm(h0, wide_ref[6:7, :], dx, dh1, dx)
    hook("g2")
    backward_near(t_hi, dx, da, probs)
    hook("g3")
    wide = wide_ref[...]
    backward_mix(wide, seg_col, rows_ref, table, dx, probs, du_ref)
    hook("g4")
    need("Fe", "Fm")
    dconv, dconv_b, dscore = backward_taps(we, wide, table, t_hi, t_low, mix, dx, da, du_ref)
    hook("g5")
    pack_smalls(sz, dconv + [dconv_b, dscore, dnorm_attn, dnorm_ffn], bias_gradient(by_off[...]), gs)
    hook("g6")
    hook("end")
    sched.rest()
    outs = [(re, re_o), (r4, r4_o), (rgu, rgu_o), (rd, rd_o), (tile, tile_o)]
    last = [pltpu.make_async_copy(a, b, out_sems.at[n + 1]) for n, (a, b) in enumerate(outs)]
    for copy in last:
        copy.start()
    for copy in [mixed_copy] + last:
        copy.wait()


def unpack_kernel(sz, mixed, re, r4, rgu, rd, tile, *outs):
    o_mixed, o_e, o_cw, o_cb, o_sw, o_na, o_q, o_k, o_v, o_o, o_rel, o_nf, o_g, o_u, o_d = outs
    o_mixed[...] = mixed[...]
    o_e[...] = re[...].astype(F32)
    for n, out in enumerate((o_q, o_k, o_v, o_o)):
        out[...] = r4[n].astype(F32)
    o_d[...] = rd[...].astype(F32)
    for n, out in enumerate((o_g, o_u)):
        for j in range(sz.ff // 128):
            for s in range(sz.shards):
                at = n * FF + 128 * (j * sz.shards + s)
                out[:, s * sz.ff + 128 * j : s * sz.ff + 128 * j + 128] = rgu[:, at : at + 128].astype(F32)
    o_cw[...] = tile[0:4, 0 : sz.d]
    for n, out in enumerate((o_cb, o_sw, o_na, o_nf)):
        out[...] = tile[4 + n, 0 : sz.d]
    o_rel[...] = tile[8, 0 : sz.rel]


def shape(dims, dtype):
    return jax.ShapeDtypeStruct(dims, dtype)


def body(shards, copies, *args):
    sz = Sizes(shards)
    vmem = pl.BlockSpec(memory_space=pltpu.VMEM)
    anywhere = pl.BlockSpec(memory_space=pl.ANY)
    n_gather = len(gather_parts(sz))
    parts = {job: part for job, (_, _, part) in reduce_parts(sz).items()}
    sems = Reduce.sems(shards, copies)
    small_in, small_out = SmallGather.sems(shards), SmallReduce.sems(shards, copies)

    def low(*dims):
        return pltpu.VMEM(dims, BF16)

    def wide(*dims):
        return pltpu.VMEM(dims, F32)

    dma = pltpu.SemaphoreType.DMA
    results = [
        shape((TOK, D), BF16),
        shape((sz.emb, D), BF16),
        shape((4, sz.d, D), BF16),
        shape((sz.d, 2 * FF), BF16),
        shape((sz.ff, D), BF16),
        shape((16, 128), F32),
    ]
    found = pl.pallas_call(
        functools.partial(step_kernel, sz, copies),
        out_shape=results,
        in_specs=[
            vmem, vmem, anywhere, vmem, vmem, vmem, vmem, anywhere, anywhere, anywhere, anywhere, vmem, vmem,
            anywhere, anywhere, anywhere, anywhere,
        ],
        out_specs=[anywhere] * len(results),
        scratch_shapes=[
            low(VOCAB, D), low(4, D, D), low(D, 2 * FF), low(FF, D),
            low(sz.emb, D), low(4, sz.d, D), low(sz.d, 2 * FF), low(sz.ff, D), wide(16, 128),
            low(shards, 16, 128), low(shards, 16, 128),
            wide(16, 128),
            low(TOK, D), low(3, TOK, D), low(HEADS, TOK, TOK), low(TOK, D), wide(TOK, D), wide(TOK, D), low(TOK, D),
            low(SPAN, 1024), low(1024, D), low(1024, D), low(TOK, 1024), wide(16, SPAN), wide(TOK, 256), wide(16, D),
            wide(16, 1024), low(TOK, D), low(TOK, D), wide(TOK, D), wide(TOK, D), low(TOK, D), low(TOK, D),
            low(2, TOK, TOK), wide(128, 1024), wide(16, 1024), wide(8, SPAN),
            dma((11,)), dma((6,)),
            dma((n_gather, Gather.sems(shards))), dma((n_gather, Gather.sems(shards))),
            dma((len(parts), sems)), dma((len(parts), sems)),
            dma((small_in,)), dma((small_in,)), dma((small_out,)), dma((small_out,)),
        ]
        + [b for job, part in parts.items() for b in Reduce.buffers(shards, copies, part, job in OUTER_FIRST)]
        + SmallReduce.buffers(shards, copies),
        compiler_params=pltpu.CompilerParams(collective_id=0, has_side_effects=True, vmem_limit_bytes=VMEM_LIMIT),
        name="layer_step",
    )(*args)
    return pl.pallas_call(
        functools.partial(unpack_kernel, sz),
        out_shape=[shape((TOK, D), BF16)] + [shape(a.shape, F32) for a in args[2:16]],
        in_specs=[vmem] * 6,
        out_specs=[vmem] * 15,
        compiler_params=pltpu.CompilerParams(vmem_limit_bytes=VMEM_LIMIT),
        name="unpack",
    )(*found)


def solution(mesh):
    both = P(("fsdp", "dp"), None)
    rows, line, taps = P("fsdp", None), P("fsdp"), P(None, "fsdp")
    weights = (rows, taps, line, line, line, rows, rows, rows, rows, line, line, rows, rows, rows)
    return jax.shard_map(
        functools.partial(body, mesh.shape["fsdp"], mesh.shape["dp"]),
        mesh=mesh,
        in_specs=(both, both) + weights + (both,),
        out_specs=(both,) + weights,
        check_vma=False,
    )
```
